32 devices in a mesh: groups: 2 (over x), dp: 8 (over z, y), tensor: 2 (over core).
Axes of the slice: x: 2, y: 2, z: 4, core: 2. Of those that a mesh axis runs over, the one named last changes fastest.
Arguments:
- hidden: bfloat16 [8192, 6144], P(('groups', 'dp'), 'tensor'), parts along dimension 0, may hold values from -320 to 320
- attn_out: bfloat16 [8192, 6144], P(('groups', 'dp'), 'tensor'), parts along dimension 0, may hold values from -6 to 6
- step_ids: int32 [8192], P(('groups', 'dp')), parts along dimension 0, may hold values from 0 to 7
- modulation: float32 [16, 2, 6144], P('groups'), parts along dimension 0, may hold values from -3 to 3
Outputs:
- hessian_qkv: float32 [2048, 6144], P(('groups', 'dp', 'tensor')), parts along dimension 0
- hessian_out: float32 [2048, 6144], P(('groups', 'dp', 'tensor')), parts along dimension 0
The draws below stay inside these ranges and needn't reach their ends.
There are 2 independent parts, one for each index of `groups`. The reference program is written for one: setup_inputs(seed, part) draws one part's arguments, and reference() takes and returns one part's arrays. A program takes and returns all parts, laid end to end along the dimension named above; each array names one. Nothing has to cross between parts.
All inputs are finite; a program needn't handle non-finite values.
Results may differ from the reference program's by a relative error of at most 0.00076.
Values may be sent and summed in bfloat16 or wider, within the bound.
No kernel may reach another device: no remote copies, remote signals or barrier semaphores. Data moves between devices by JAX's collectives and lax.ppermute only.
A program may use at most 128 MiB of HBM per device.

```python
import jax
import jax.numpy as jnp
import numpy as np
from jax import lax

D = 6144
ROW_DEV = 512
STEPS = 8
TOKENS = 4096
N_DP = 8
N_TENSOR = 2


def draw_hidden(key, part):
    key = jax.random.fold_in(key, 11)
    key_scale, key_offset, key_rows, key_base = jax.random.split(key, 4)
    column = jnp.arange(D, dtype=jnp.float32)
    rising = 0.5 + 2.0 * column / D
    column_scale = jnp.exp(jax.random.uniform(key_scale, (D,), jnp.float32, 0.0, jnp.log(10.0))) * rising
    offset = jax.random.truncated_normal(key_offset, -3.0, 3.0, (D,), jnp.float32)
    row_scale = jnp.exp(jax.random.uniform(key_rows, (TOKENS, 1), jnp.float32, jnp.log(0.3), jnp.log(3.0)))
    base = jax.random.truncated_normal(key_base, -4.0, 4.0, (TOKENS, D), jnp.float32)
    return ((base * column_scale + offset) * row_scale).astype(jnp.bfloat16)


def with_ends(entries, own_key, low, largest):
    longest = entries.shape.index(max(entries.shape))
    spots = []
    for shift in (0, 1):
        where = [jax.random.randint(jax.random.fold_in(own_key, axis), (), 0, length) for axis, length in enumerate(entries.shape)]
        where[longest] = (where[longest] + shift) % entries.shape[longest]
        spots.append(tuple(where))
    return entries.at[spots[0]].set(low).at[spots[1]].set(largest)


def with_spikes(values, key, source, target, parts, factor):
    owner, partner = [(jnp.arange(values.shape[axis_at]) // (values.shape[axis_at] // parts)).reshape([-1 if axis == axis_at else 1 for axis in range(values.ndim)]) for axis_at in (source, target)]
    chosen = jax.random.permutation(key, parts)[partner]
    strong = (owner == chosen) | (owner == (partner + parts // 2) % parts)
    return jnp.where(strong, factor * values, values)


def block_scale(stream_key, dims, shards, least, largest):
    gain = 1.0
    for axis_at, parts in shards:
        heights = jax.random.uniform(jax.random.fold_in(jax.random.fold_in(stream_key, 6), axis_at), (parts,), jnp.float32, least / len(shards), largest / len(shards))
        gain = gain * jnp.repeat(jnp.exp(heights), dims[axis_at] // parts).reshape((-1,) + (1,) * (len(dims) - 1 - axis_at))
    return gain


def centred(stream_key, shape, deviation, reach, cuts=(), held_as=jnp.bfloat16):
    result = deviation * jax.random.normal(stream_key, shape, jnp.float32)
    if cuts:
        result = result * block_scale(stream_key, shape, cuts, -0.22, 0.18)
    return jnp.clip(result, -reach, reach).astype(held_as)


def heavy_noise(own_key, dims, scale, most, cuts, heavy, held_as=jnp.bfloat16):
    array = scale * jax.random.normal(own_key, dims, jnp.float32)
    if cuts:
        array = array * block_scale(own_key, dims, cuts, -0.22, 0.18)
    return jnp.clip(with_spikes(array, jax.random.fold_in(own_key, 3), *heavy), -most, most).astype(held_as)


def setup_inputs(seed: int = 0, part: int = 0) -> dict:
    key_list = jax.random.split(jax.random.key(seed), 5)
    part_splits = jax.random.split(jax.random.fold_in(key_list[4], part), 5)
    hidden = draw_hidden(jax.random.fold_in(jax.random.fold_in(key_list[4], part), 71), part)
    attn_out = heavy_noise(part_splits[1], (TOKENS, D), 1.0, 6.0, ((0, 8), (1, 2)), (0, 1, 8, 2.0))
    step_ids = with_ends(jax.random.randint(part_splits[2], (TOKENS,), 0, STEPS), jax.random.fold_in(part_splits[2], 1), 0, STEPS - 1).astype(jnp.int32)
    modulation = centred(part_splits[3], (STEPS, 2, D), 0.5, 3.0, (), jnp.float32)
    return dict(hidden=hidden, attn_out=attn_out, step_ids=step_ids, modulation=modulation)


epsilon = 1e-06

def window_features(rows_dev, width, parts_dp, parts_tp):
    block = rows_dev // parts_dp
    index = np.arange(rows_dev * parts_tp)
    dp_part = index // (parts_tp * block)
    tp_part = index // block % parts_tp
    within = index % block
    return (tp_part * (width // parts_tp) + dp_part * block + within).astype(np.int32)

def reference(hidden, attn_out, step_ids, modulation):
    values = hidden.astype(jnp.float32)
    mean = lax.optimization_barrier(jnp.mean(values, axis=1, keepdims=True))
    meansq = lax.optimization_barrier(jnp.mean(values * values, axis=1, keepdims=True))
    normed = (values - mean) * lax.rsqrt(meansq - mean * mean + epsilon)
    scale = modulation[step_ids, 0, :]
    shift = modulation[step_ids, 1, :]
    modulated = (normed * (1.0 + scale) + shift).astype(jnp.bfloat16)
    picked_index = jnp.asarray(window_features(ROW_DEV, D, N_DP, N_TENSOR))
    factor = 2.0 / TOKENS
    picked_qkv = modulated[:, picked_index]
    hessian_qkv = jnp.dot(picked_qkv.T, modulated, preferred_element_type=jnp.float32) * factor
    picked_out = attn_out[:, picked_index]
    hessian_out = jnp.dot(picked_out.T, attn_out, preferred_element_type=jnp.float32) * factor
    return (hessian_qkv, hessian_out)
```

```python
import functools

import jax
import jax.numpy as jnp
from jax import lax
from jax.experimental import pallas as pl
from jax.experimental.pallas import tpu as pltpu
from jax.sharding import PartitionSpec as P

ROW_DEV = 512
LANES = 256


epsilon = 1e-06


def lookup_table(step_ids, table):
    steps = table.shape[0]
    columns = table.shape[2]
    onehot = (step_ids[:, None] == jnp.arange(steps, dtype=jnp.int32)[None, :]).astype(jnp.float32)
    looked = jnp.dot(onehot, table.reshape(steps, 2 * columns), precision=lax.Precision.HIGHEST)
    return (looked[:, :columns], looked[:, columns:])


def gram_rows(window, full):
    return lax.dot_general(
        window, full, (((0,), (0,)), ((), ())), preferred_element_type=jnp.float32
    )


def plain_body(hidden, attn_out, step_ids, modulation):
    token_count = hidden.shape[0]
    local_width = hidden.shape[1]
    parts_tp = lax.axis_size("tensor")
    parts_dp = lax.axis_size("dp")
    width = local_width * parts_tp
    rows_dev = ROW_DEV
    factor = 2.0 / (token_count * parts_dp)
    column_start = lax.axis_index("tensor") * local_width
    local_table = lax.dynamic_slice_in_dim(modulation, column_start, local_width, 2)
    scale, shift = lookup_table(step_ids, local_table)
    values = hidden.astype(jnp.float32)
    moments = lax.psum((jnp.sum(values, axis=1), jnp.sum(values * values, axis=1)), "tensor")
    mean = (moments[0] / width)[:, None]
    meansq = (moments[1] / width)[:, None]
    normed = (values - mean) * lax.rsqrt(meansq - mean * mean + epsilon)
    local_mod = (normed * (1.0 + scale) + shift).astype(jnp.bfloat16)
    full_mod, full_attn = (
        lax.all_gather(local_mod, "tensor", axis=1, tiled=True),
        lax.all_gather(attn_out, "tensor", axis=1, tiled=True),
    )
    part_qkv = gram_rows(local_mod[:, :rows_dev], full_mod)
    part_out = gram_rows(attn_out[:, :rows_dev], full_attn)
    summed_qkv, summed_out = (
        lax.psum_scatter(part_qkv, "dp", scatter_dimension=0, tiled=True),
        lax.psum_scatter(part_out, "dp", scatter_dimension=0, tiled=True),
    )
    return (summed_qkv * factor, summed_out * factor)


def swap(size, mask=1):
    return [(i, i ^ mask) for i in range(size)]


def cut(values, start, size, axis):
    return lax.dynamic_slice_in_dim(values, start, size, axis)


def half16(values):
    return values.astype(jnp.float16)


def full32(values):
    return values.astype(jnp.float32)


FREE = pl.CostEstimate(flops=0, bytes_accessed=0, transcendentals=0)


def gridded(kernel, indices, grid, in_specs, out_specs, out_shape, *operands):
    return pl.pallas_call(
        kernel,
        grid_spec=pltpu.PrefetchScalarGridSpec(
            num_scalar_prefetch=1, grid=(grid,), in_specs=in_specs, out_specs=out_specs
        ),
        out_shape=out_shape,
        cost_estimate=FREE,
        compiler_params=pltpu.CompilerParams(vmem_limit_bytes=32 << 20),
    )(indices, *operands)


def vector(*entries):
    return jnp.stack([jnp.asarray(entry, jnp.int32) for entry in entries])


def pick_kernel(at, source, out):
    out[...] = source[...]


def pick(source, *blocks):
    tokens = source.shape[0]
    return gridded(
        pick_kernel,
        vector(*blocks),
        len(blocks),
        [pl.BlockSpec((tokens, LANES), lambda i, at: (0, at[i]))],
        pl.BlockSpec((tokens, LANES), lambda i, at: (0, i)),
        jax.ShapeDtypeStruct((tokens, LANES * len(blocks)), source.dtype),
        source,
    )


def turn_kernel(at, source, out):
    out[...] = source[...].T


def turn(source, blocks):
    tokens = source.shape[0]
    size = ROW_DEV // len(blocks)
    return gridded(
        turn_kernel,
        vector(*blocks),
        len(blocks),
        [pl.BlockSpec((tokens, size), lambda i, at: (0, at[i]))],
        pl.BlockSpec((size, tokens), lambda i, at: (i, 0)),
        jax.ShapeDtypeStruct((ROW_DEV, tokens), source.dtype),
        source,
    )


def store_sums(total, out, peak):
    out[...] = total
    peak[...] = jnp.broadcast_to(jnp.max(jnp.abs(total), axis=0, keepdims=True), peak.shape)


def gram_kernel(at, rows, columns, out, peak):
    store_sums(jnp.dot(rows[...], columns[...], preferred_element_type=jnp.float32), out, peak)


def gram_two_kernel(at, rows, columns, other_rows, other_columns, out, peak):
    total = jnp.dot(rows[...], columns[...], preferred_element_type=jnp.float32)
    total = total + jnp.dot(other_rows[...], other_columns[...], preferred_element_type=jnp.float32)
    store_sums(total, out, peak)


def gram(rows, columns, blocks, other=None):
    tokens = columns.shape[0]
    in_specs = [
        pl.BlockSpec((ROW_DEV, tokens), lambda i, at: (0, 0)),
        pl.BlockSpec((tokens, LANES), lambda i, at: (0, at[i])),
    ]
    operands = [rows, columns]
    skip = 0
    if other is not None:
        other_rows, other_columns, skip = other
        in_specs += [
            pl.BlockSpec((ROW_DEV, tokens), lambda i, at: (0, 0)),
            pl.BlockSpec((tokens, LANES), lambda i, at: (0, i + skip)),
        ]
        operands += [other_rows, other_columns]
    width = LANES * len(blocks)
    return gridded(
        gram_kernel if other is None else gram_two_kernel,
        vector(*blocks),
        len(blocks),
        in_specs,
        [pl.BlockSpec((ROW_DEV, LANES), lambda i, at: (0, i)), pl.BlockSpec((8, LANES), lambda i, at: (0, i))],
        [
            jax.ShapeDtypeStruct((ROW_DEV, width), jnp.float32),
            jax.ShapeDtypeStruct((8, width), jnp.float32),
        ],
        *operands,
    )


def modulate_kernel(ids, values, mean, gain, scale_table, shift_table, out):
    tokens = values.shape[0]
    steps = scale_table.shape[0]
    place = lax.broadcasted_iota(jnp.int32, (tokens, 3 * steps), 1)
    onehot = (ids[...] == lax.rem(place, steps)).astype(jnp.bfloat16)

    def lookup(table):
        entries = table[...]
        pieces = []
        for _ in range(3):
            piece = entries.astype(jnp.bfloat16).astype(jnp.float32)
            entries = entries - piece
            pieces.append(piece)
        split = jnp.concatenate(pieces, axis=0).astype(jnp.bfloat16)
        return jnp.dot(onehot, split, preferred_element_type=jnp.float32)

    normed = (values[...].astype(jnp.float32) - mean[...]) * gain[...]
    out[...] = (normed * (1.0 + lookup(scale_table)) + lookup(shift_table)).astype(jnp.bfloat16)


def modulate(values, mean, gain, step_ids, table):
    tokens, width = values.shape
    steps = table.shape[0]
    size = 2 * LANES
    whole = pl.BlockSpec((tokens, 1), lambda i: (0, 0))
    columns = pl.BlockSpec((tokens, size), lambda i: (0, i))
    entries = pl.BlockSpec((steps, size), lambda i: (0, i))
    return pl.pallas_call(
        modulate_kernel,
        grid=(width // size,),
        in_specs=[whole, columns, whole, whole, entries, entries],
        out_specs=columns,
        out_shape=jax.ShapeDtypeStruct(values.shape, jnp.bfloat16),
        cost_estimate=FREE,
        compiler_params=pltpu.CompilerParams(vmem_limit_bytes=32 << 20),
    )(step_ids[:, None], values, mean, gain, table[:, 0], table[:, 1])


INWARD = [(0, 2), (1, 3), (6, 4), (7, 5)]
MIDDLE = [(2, 4), (3, 5), (4, 2), (5, 3)]
OUTWARD = [(2, 0), (3, 1), (4, 6), (5, 7)]


def packed(values, peak):
    exponent = jnp.ceil(jnp.log2(jnp.maximum(peak, 1e-30))) - 15.0
    scaled = values * jnp.exp2(-exponent)
    tail = jnp.broadcast_to(exponent, (16, values.shape[1]))
    return half16(jnp.concatenate([scaled, tail], axis=0))


def unit(message):
    return jnp.exp2(full32(message[-1:]))


def unpacked(message, first, last):
    return full32(message[first:last]) * unit(message)


def reach(message):
    return 32768.0 * unit(message)


def pipeline(count, make_part, stage, early):
    side = lax.axis_index("dp") % 2
    place = lax.axis_index("dp") // 2
    outer = (place == 0) | (place == 3)
    part, peak, sent1, came1, came2, came3, came4, owned = {}, {}, {}, {}, {}, {}, {}, {}
    done = []

    def begin(k, raw):
        part[k], peak[k] = make_part(k, raw)
        peak[k] = peak[k][:1]
        block = part[k].shape[0] // 4
        sent1[k] = packed(part[k][: 3 * block], peak[k])
        came1[k] = lax.ppermute(sent1[k], "dp", INWARD)

    begin(0, stage(0))
    begin(1, stage(1))
    extra = early(sent1[1])
    for k in range(count + 3):
        held = [group[j] for group, j in ((came1, k), (came2, k - 1), (came3, k - 2), (came4, k - 3)) if 0 <= j < count]
        if k + 1 < count:
            held.append(sent1[k + 1])
        if k == 0:
            held.append(extra)
        held = list(lax.optimization_barrier(tuple(held)))
        if k == 0:
            early(None, held.pop())
        ahead = []
        if k < count:
            came1[k] = held.pop(0)
            block = part[k].shape[0] // 4
            total = part[k][: 2 * block] + unpacked(came1[k], 0, 2 * block)
            sent = packed(total, peak[k] + reach(came1[k]))
            ahead.append(sent)
            came2[k] = lax.ppermute(sent, "dp", MIDDLE)
        if 0 <= k - 1 < count:
            j = k - 1
            came2[j] = held.pop(0)
            block = part[j].shape[0] // 4
            total = part[j][2 * block : 3 * block] + unpacked(came2[j], block, 2 * block)
            sent = packed(total, peak[j] + reach(came2[j]))
            ahead.append(sent)
            came3[j] = lax.ppermute(sent, "dp", OUTWARD)
        if 0 <= k - 2 < count:
            j = k - 2
            came3[j] = held.pop(0)
            block = part[j].shape[0] // 4
            total = part[j][3 * block :] + unpacked(came1[j], 2 * block, 3 * block)
            total = total + unpacked(came2[j], 0, block) + unpacked(came3[j], 0, block)
            more = jnp.where(outer, reach(came3[j]), reach(came1[j]) + reach(came2[j]))
            own = block // 2
            owned[j] = cut(total, side * own, own, 0)
            sent = packed(cut(total, (1 - side) * own, own, 0), peak[j] + more)
            ahead.append(sent)
            came4[j] = lax.ppermute(sent, "dp", swap(8))
        if 0 <= k - 3 < count:
            j = k - 3
            done.append((owned[j], unpacked(held.pop(0), 0, owned[j].shape[0])))
        if k + 2 < count:
            raw, _ = lax.optimization_barrier((stage(k + 2), tuple(ahead)))
            begin(k + 2, raw)
    return done


def in_order(own, other):
    side = lax.axis_index("dp") % 2
    return jnp.where(side == 0, own, other), jnp.where(side == 0, other, own)


def assemble(done, shared, scale):
    core = lax.axis_index("tensor")
    half = ROW_DEV // 2
    cores = []
    for which in range(2):
        mine = done[which::2]
        pieces = []
        if shared:
            pieces.append(mine[0][0] + mine[0][1])
            mine = mine[1:]
        ordered = [in_order(*pair) for pair in mine]
        head = [ordered[0][0][:, :half], ordered[0][1][:, :half]]
        ordered[0] = (ordered[0][0][:, half:], ordered[0][1][:, half:])
        pieces = head + pieces + [pair[0] for pair in ordered] + [pair[1] for pair in ordered]
        cores.append(jnp.concatenate(pieces, axis=1))
    left = jnp.where(core == 0, cores[0], cores[1])
    right = jnp.where(core == 0, cores[1], cores[0])
    return jnp.concatenate([left, right], axis=1) * scale


def body(hidden, attn_out, step_ids, modulation):
    token_count = hidden.shape[0]
    local_width = hidden.shape[1]
    parts_tp = lax.axis_size("tensor")
    dp = lax.axis_size("dp")
    width = local_width * parts_tp
    tokens = token_count * dp
    factor = 2.0 / tokens
    column_start = lax.axis_index("tensor") * local_width
    local_table = lax.dynamic_slice_in_dim(modulation, column_start, local_width, 2)
    core_swap = swap(2)
    side = lax.axis_index("dp") % 2
    place = lax.axis_index("dp") // 2
    blocks = local_width // LANES
    store = {}

    low = place < 2
    order = [jnp.where(low, 2, 1), jnp.where(low, 3, 0), place ^ 1, place]
    arrived = [jnp.where(index // 2 == side, 2 + index % 2, index % 2) for index in order]

    def owned_blocks(which, common):
        rest = (blocks - 2 - common) // 2
        return [which] + [2 + common + which * rest + i for i in range(rest)]

    common = 4
    attn_mine = owned_blocks(side, common)
    attn_theirs = owned_blocks(1 - side, common)
    qkv_mine = owned_blocks(side, 0)
    qkv_theirs = owned_blocks(1 - side, 0)
    first = 4

    shared = [2 + i for i in range(common)]
    attn_far = lax.ppermute(attn_out, "tensor", core_swap)
    attn_rows = turn(attn_out, order)
    attn_pair = lax.ppermute(pick(attn_out, side, *attn_theirs), "dp", swap(dp))

    def early(earlier, result=None):
        if result is not None:
            store["mod"] = result
            return
        values, _ = lax.optimization_barrier((hidden, earlier))
        values32 = values.astype(jnp.float32)
        moments = lax.psum((jnp.sum(values32, axis=1), jnp.sum(values32 * values32, axis=1)), "tensor")
        mean = (moments[0] / width)[:, None]
        meansq = (moments[1] / width)[:, None]
        gain = lax.rsqrt(meansq - mean * mean + epsilon)
        return modulate(values, mean, gain, step_ids, local_table)

    def stage(k):
        if k == 0:
            return attn_out
        if k == 1:
            return attn_far
        if k == 2:
            return attn_pair, store["mod"]
        if k in (4, 6):
            return store["pair"]
        return store["far"]

    def make_part(k, raw):
        if k < 2:
            return gram(attn_rows, raw, shared)
        if k == 2:
            pair, mod = raw
            store["far"] = lax.ppermute(pair, "tensor", core_swap)
            store["other"] = turn(pair, arrived)
            store["mod"] = mod
            store["pair"] = lax.ppermute(pick(mod, side, *qkv_theirs[:first]), "dp", swap(dp))
            store["mod_far"] = lax.ppermute(mod, "tensor", core_swap)
            store["rows"] = turn(mod, order)
            return gram(attn_rows, attn_out, attn_mine, (store["other"], pair, 1))
        if k == 3:
            return gram(attn_rows, attn_far, attn_mine, (store["other"], raw, 1))
        if k == 4:
            store["far"] = lax.ppermute(raw, "tensor", core_swap)
            store["other"] = turn(raw, arrived)
            mod, _ = lax.optimization_barrier((store["mod"], raw))
            store["pair"] = lax.ppermute(pick(mod, *qkv_theirs[first:]), "dp", swap(dp))
            return gram(store["rows"], store["mod"], qkv_mine[:first], (store["other"], raw, 1))
        if k == 5:
            return gram(store["rows"], store["mod_far"], qkv_mine[:first], (store["other"], raw, 1))
        if k == 6:
            store["far"] = lax.ppermute(raw, "tensor", core_swap)
            return gram(store["rows"], store["mod"], qkv_mine[first:], (store["other"], raw, 0))
        return gram(store["rows"], store["mod_far"], qkv_mine[first:], (store["other"], raw, 0))

    done = pipeline(8, make_part, stage, early)
    out_rows = assemble(done[:4], True, factor)
    qkv_rows = assemble(done[4:], False, factor)
    return (qkv_rows, out_rows)


def solution(mesh):
    lined = mesh.shape["dp"] == 8 and mesh.shape["tensor"] == 2
    return jax.shard_map(
        body if lined else plain_body,
        mesh=mesh,
        in_specs=(
            P(("groups", "dp"), "tensor"),
            P(("groups", "dp"), "tensor"),
            P(("groups", "dp")),
            P("groups", None, None),
        ),
        out_specs=(P(("groups", "dp", "tensor"), None), P(("groups", "dp", "tensor"), None)),
        check_vma=False,
    )
```

```python
import functools

import jax
import jax.numpy as jnp
from jax import lax
from jax.experimental import pallas as pl
from jax.experimental.pallas import tpu as pltpu
from jax.sharding import PartitionSpec as P

ROW_DEV = 512
LANES = 256


epsilon = 1e-06
VMEM = 16 << 20
TAIL = 16
LAG = 2
LATER = (2, 3, 4, 5, 6, 7)
LAST = 8
GATE = 1
CHUNKS = [[("shared", False, 0, 4)], [("shared", True, 0, 4)], [("attn", False, 0, 4)], [("attn", True, 0, 4)], [("qkv", False, 0, 4)], [("qkv", True, 0, 4)], [("qkv", False, 4, 2)], [("qkv", True, 4, 2)]]
PIECES = (5, 2)


def lookup_table(step_ids, table):
    steps = table.shape[0]
    columns = table.shape[2]
    onehot = (step_ids[:, None] == jnp.arange(steps, dtype=jnp.int32)[None, :]).astype(jnp.float32)
    looked = jnp.dot(onehot, table.reshape(steps, 2 * columns), precision=lax.Precision.HIGHEST)
    return (looked[:, :columns], looked[:, columns:])


def gram_rows(window, full):
    return lax.dot_general(
        window, full, (((0,), (0,)), ((), ())), preferred_element_type=jnp.float32
    )


def plain_body(hidden, attn_out, step_ids, modulation):
    token_count = hidden.shape[0]
    local_width = hidden.shape[1]
    parts_tp = lax.axis_size("tensor")
    parts_dp = lax.axis_size("dp")
    width = local_width * parts_tp
    rows_dev = ROW_DEV
    factor = 2.0 / (token_count * parts_dp)
    column_start = lax.axis_index("tensor") * local_width
    local_table = lax.dynamic_slice_in_dim(modulation, column_start, local_width, 2)
    scale, shift = lookup_table(step_ids, local_table)
    values = hidden.astype(jnp.float32)
    moments = lax.psum((jnp.sum(values, axis=1), jnp.sum(values * values, axis=1)), "tensor")
    mean = (moments[0] / width)[:, None]
    meansq = (moments[1] / width)[:, None]
    normed = (values - mean) * lax.rsqrt(meansq - mean * mean + epsilon)
    local_mod = (normed * (1.0 + scale) + shift).astype(jnp.bfloat16)
    full_mod, full_attn = (
        lax.all_gather(local_mod, "tensor", axis=1, tiled=True),
        lax.all_gather(attn_out, "tensor", axis=1, tiled=True),
    )
    part_qkv = gram_rows(local_mod[:, :rows_dev], full_mod)
    part_out = gram_rows(attn_out[:, :rows_dev], full_attn)
    summed_qkv, summed_out = (
        lax.psum_scatter(part_qkv, "dp", scatter_dimension=0, tiled=True),
        lax.psum_scatter(part_out, "dp", scatter_dimension=0, tiled=True),
    )
    return (summed_qkv * factor, summed_out * factor)


def swap(size, mask=1):
    return [(i, i ^ mask) for i in range(size)]


def cut(values, start, size, axis):
    return lax.dynamic_slice_in_dim(values, start, size, axis)


FREE = pl.CostEstimate(flops=0, bytes_accessed=0, transcendentals=0)


def gridded(kernel, indices, grid, in_specs, out_specs, out_shape, *operands):
    return pl.pallas_call(
        kernel,
        grid_spec=pltpu.PrefetchScalarGridSpec(
            num_scalar_prefetch=1, grid=(grid,), in_specs=in_specs, out_specs=out_specs
        ),
        out_shape=out_shape,
        cost_estimate=FREE,
        compiler_params=pltpu.CompilerParams(vmem_limit_bytes=VMEM),
    )(indices, *operands)


def pick_kernel(at, source, out):
    out[...] = source[...]


def pick(plan, source, first, count):
    tokens = source.shape[0]
    return gridded(
        pick_kernel,
        plan,
        count,
        [pl.BlockSpec((tokens, LANES), lambda i, at: (0, at[first + i]))],
        pl.BlockSpec((tokens, LANES), lambda i, at: (0, i)),
        jax.ShapeDtypeStruct((tokens, LANES * count), source.dtype),
        source,
    )


def turn_kernel(at, source, out):
    out[...] = source[...].T


def turn(plan, source, first):
    tokens = source.shape[0]
    size = ROW_DEV // 4
    return gridded(
        turn_kernel,
        plan,
        4,
        [pl.BlockSpec((tokens, size), lambda i, at: (0, at[first + i]))],
        pl.BlockSpec((size, tokens), lambda i, at: (i, 0)),
        jax.ShapeDtypeStruct((ROW_DEV, tokens), source.dtype),
        source,
    )


def store_coded(total, message):
    rows = total.shape[0]
    peak = jnp.max(jnp.abs(total), axis=0, keepdims=True)
    power = jnp.ceil(jnp.log2(jnp.maximum(peak, 1e-30))) - 15.0
    codes = jnp.clip(jnp.round(total * jnp.exp2(-power)), -32767.0, 32767.0)
    message[:rows, :] = codes.astype(jnp.int32).astype(jnp.int16)
    tail = jnp.broadcast_to(power, (TAIL, total.shape[1]))
    message[rows:, :] = tail.astype(jnp.int32).astype(jnp.int16)


def decoded(message, first, last):
    power = message[message.shape[0] - TAIL :, :].astype(jnp.int32).astype(jnp.float32)[:1]
    return message[first:last, :].astype(jnp.int32).astype(jnp.float32) * jnp.exp2(power)


def chosen_piece(step, starts, pieces):
    values = pieces[0][...]
    for start, piece in zip(starts[1:], pieces[1:]):
        values = jnp.where(step < start, values, piece[...])
    return values


def gram_kernel(starts, at, rows, *refs):
    own, message = refs[-2:]
    step = pl.program_id(0)
    mine = len(starts[0])
    total = jnp.dot(rows[...], chosen_piece(step, starts[0], refs[:mine]), preferred_element_type=jnp.float32)
    if starts[1]:
        columns = chosen_piece(step, starts[1], refs[mine + 1 : -2])
        total = total + jnp.dot(refs[mine][...], columns, preferred_element_type=jnp.float32)
    sent = message.shape[0] - TAIL
    own[...] = total[sent:]
    store_coded(total[:sent], message)


def gram(plan, rows, columns, other_rows=None, other_columns=()):
    tokens = rows.shape[1]
    whole = pl.BlockSpec((ROW_DEV, tokens), lambda i, at: (0, 0))
    in_specs, operands = [whole], [rows]
    starts = ([], [])
    for group, pieces in enumerate((columns, other_columns)):
        if group == 1 and pieces:
            in_specs.append(whole)
            operands.append(other_rows)
        start = 0
        for array, base, held in pieces:

            def place(i, at, listed=group == 0, base=base, held=held, start=start):
                index = jnp.clip(i - start, 0, held - 1) + base
                return (0, at[index] if listed else index)

            in_specs.append(pl.BlockSpec((tokens, LANES), place))
            operands.append(array)
            starts[group].append(start)
            start += held
    count = sum(held for _, _, held in columns)
    width = LANES * count
    own = ROW_DEV // 2
    sent = ROW_DEV - own + TAIL
    return gridded(
        functools.partial(gram_kernel, tuple(map(tuple, starts))),
        plan,
        count,
        in_specs,
        [pl.BlockSpec((own, LANES), lambda i, at: (0, i)), pl.BlockSpec((sent, LANES), lambda i, at: (0, i))],
        [jax.ShapeDtypeStruct((own, width), jnp.float32), jax.ShapeDtypeStruct((sent, width), jnp.int16)],
        *operands,
    )


def blocked(kernel, width, inputs, outputs):
    size = min(width, 2 * LANES)
    return pl.pallas_call(
        kernel,
        grid=(width // size,),
        in_specs=[pl.BlockSpec((rows, size), lambda i, at=at: (at, i)) for _, rows, at in inputs],
        out_specs=[pl.BlockSpec((rows, size), lambda i: (0, i)) for rows, _ in outputs],
        out_shape=[jax.ShapeDtypeStruct((rows, width), dtype) for rows, dtype in outputs],
        cost_estimate=FREE,
        compiler_params=pltpu.CompilerParams(vmem_limit_bytes=VMEM),
    )(*[array for array, _, _ in inputs])


def add_kernel(own, came, message):
    rows = own.shape[0]
    store_coded(own[...] + decoded(came, 0, rows), message)


def add_sums(own, came):
    rows = own.shape[0] // 2
    inputs = [(own, rows, 0), (came, came.shape[0], 0)]
    return blocked(add_kernel, own.shape[1], inputs, [(rows + TAIL, jnp.int16)])[0]


def total_kernel(own, came1, came2, mine, message):
    rows = own.shape[0]
    total = own[...] + decoded(came1, rows, 2 * rows) + decoded(came2, 0, rows)
    side = lax.rem(lax.axis_index("dp"), 2)
    half = rows // 2
    low, high = total[:half], total[half:]
    mine[...] = jnp.where(side == 0, low, high)
    store_coded(jnp.where(side == 0, high, low), message)


def total_sums(own, came1, came2):
    rows = own.shape[0] // 2
    inputs = [(own, rows, 1), (came1, came1.shape[0], 0), (came2, came2.shape[0], 0)]
    outputs = [(rows // 2, jnp.float32), (rows // 2 + TAIL, jnp.int16)]
    return blocked(total_kernel, own.shape[1], inputs, outputs)


def token_columns(rows):
    full = jnp.concatenate([rows, jnp.zeros((8 - rows.shape[0], rows.shape[1]), rows.dtype)], axis=0)
    return full.T


def chosen_rows(ids, steps, kind, repeat):
    place = lax.broadcasted_iota(jnp.int32, (ids.shape[0], repeat * 2 * steps), 1)
    return (2.0 * ids + kind).astype(jnp.int32) == lax.rem(place, 2 * steps)


def stats_kernel(hidden, moments):
    values = hidden[...].astype(jnp.float32)
    total = jnp.sum(values, axis=1, keepdims=True)
    squares = jnp.sum(values * values, axis=1, keepdims=True)
    lane = lax.broadcasted_iota(jnp.int32, (values.shape[0], 128), 1)
    moments[...] = jnp.where(lane == 0, total, jnp.where(lane == 1, squares, 0.0)).T[:8]


def stats(hidden):
    tokens, width = hidden.shape
    size = tokens // 4
    return pl.pallas_call(
        stats_kernel,
        grid=(4,),
        in_specs=[pl.BlockSpec((size, width), lambda i: (i, 0))],
        out_specs=pl.BlockSpec((8, size), lambda i: (0, i)),
        out_shape=jax.ShapeDtypeStruct((8, tokens), jnp.float32),
        cost_estimate=FREE,
        compiler_params=pltpu.CompilerParams(vmem_limit_bytes=VMEM),
    )(hidden)


def modulate_kernel(width, at, ids, moments, values, table, out):
    steps = table.shape[0] // 2
    turned = token_columns(jnp.concatenate([moments[...][:2], ids[...].astype(jnp.float32)], axis=0))
    mean = turned[:, :1] * (1.0 / width)
    meansq = turned[:, 1:2] * (1.0 / width)
    gain = lax.rsqrt(meansq - mean * mean + epsilon)
    entries = table[...]
    pieces = []
    for _ in range(3):
        piece = entries.astype(jnp.bfloat16).astype(jnp.float32)
        entries = entries - piece
        pieces.append(piece)
    split = jnp.concatenate(pieces, axis=0).astype(jnp.bfloat16)

    def lookup(kind):
        onehot = chosen_rows(turned[:, 2:3], steps, kind, 3).astype(jnp.bfloat16)
        return jnp.dot(onehot, split, preferred_element_type=jnp.float32)

    normed = (values[...].astype(jnp.float32) - mean) * gain
    out[...] = (normed * (1.0 + lookup(0)) + lookup(1)).astype(jnp.bfloat16)


def modulate(plan, at_core, step_ids, moments, values, table, width):
    tokens, local_width = values.shape
    size = 2 * LANES
    count = local_width // size
    columns = pl.BlockSpec((tokens, size), lambda i, at: (0, i))
    return gridded(
        functools.partial(modulate_kernel, width),
        plan,
        count,
        [
            pl.BlockSpec((1, tokens), lambda i, at: (0, 0)),
            pl.BlockSpec((8, tokens), lambda i, at: (0, 0)),
            columns,
            pl.BlockSpec((table.shape[0], size), lambda i, at: (0, at[at_core] * count + i)),
        ],
        columns,
        jax.ShapeDtypeStruct(values.shape, jnp.bfloat16),
        step_ids,
        moments,
        values,
        table,
    )


def pipeline(count, make_part, stage, hooks, later, finish):
    own, sent1, came1, came2, came3, owned = {}, {}, {}, {}, {}, {}
    due2, due3 = {}, {}
    for j in range(count):
        due2[j] = max(j + 1, min(j + (LAG if j < LAST else 1), count))
        due3[j] = due2[j] + 1

    def begin(k, raw):
        own[k], sent1[k] = make_part(k, raw)
        came1[k] = lax.ppermute(sent1[k], "dp", swap(8, 2))

    begin(0, stage(0))
    begin(1, stage(1))
    for k in range(max(due3.values()) + 1):
        now2 = [j for j in range(count) if due2[j] == k]
        now3 = [j for j in range(count) if due3[j] == k]
        wanted = {"came2": [came2[j] for j in now2], "came3": [came3[j] for j in now3]}
        if k < count:
            wanted["came1"] = came1[k]
        if k + 1 < count:
            wanted["sent1"] = sent1[k + 1]
        if k in hooks:
            wanted["more"] = hooks[k][0]()
        wanted = lax.optimization_barrier(wanted)
        if k in hooks:
            hooks[k][1](wanted["more"])
        if k + 2 < count and k + 2 not in later:
            raw, _ = lax.optimization_barrier((stage(k + 2), wanted["came1"]))
            begin(k + 2, raw)
            wanted, _ = lax.optimization_barrier((wanted, sent1[k + 2]))
        ahead = []
        if k < count:
            came1[k] = wanted["came1"]
            sent = add_sums(own[k], came1[k])
            ahead.append(sent)
            came2[k] = lax.ppermute(sent, "dp", swap(8, 4))
        for j, came in zip(now2, wanted["came2"]):
            owned[j], sent = total_sums(own[j], came1[j], came)
            ahead.append(sent)
            came3[j] = lax.ppermute(sent, "dp", swap(8))
        for j, came in zip(now3, wanted["came3"]):
            finish(j, owned[j], came)
        if k + 2 < count and k + 2 in later:
            raw, _ = lax.optimization_barrier((stage(k + 2), tuple(ahead)))
            begin(k + 2, raw)


def unpacked(message):
    rows = message.shape[0] - TAIL
    return message[:rows].astype(jnp.float32) * jnp.exp2(message[rows : rows + 1].astype(jnp.float32))


def in_order(own, other):
    side = lax.axis_index("dp") % 2
    return jnp.where(side == 0, own, other), jnp.where(side == 0, other, own)


def assemble(done, shared, scale):
    core = lax.axis_index("tensor")
    half = ROW_DEV // 2
    cores = []
    for which in range(2):
        mine = done[which::2]
        pieces = []
        if shared:
            pieces.append(mine[0][0] + mine[0][1])
            mine = mine[1:]
        ordered = [in_order(*pair) for pair in mine]
        head = [ordered[0][0][:, :half], ordered[0][1][:, :half]]
        ordered[0] = (ordered[0][0][:, half:], ordered[0][1][:, half:])
        pieces = head + pieces + [pair[0] for pair in ordered] + [pair[1] for pair in ordered]
        cores.append(jnp.concatenate(pieces, axis=1))
    left = jnp.where(core == 0, cores[0], cores[1])
    right = jnp.where(core == 0, cores[1], cores[0])
    return jnp.concatenate([left, right], axis=1) * scale


def body(hidden, attn_out, step_ids, modulation):
    token_count = hidden.shape[0]
    local_width = hidden.shape[1]
    parts_tp = lax.axis_size("tensor")
    dp = lax.axis_size("dp")
    width = local_width * parts_tp
    tokens = token_count * dp
    factor = 2.0 / tokens
    core_swap = swap(2)
    side = lax.axis_index("dp") % 2
    place = lax.axis_index("dp") // 2
    blocks = local_width // LANES
    store = {}

    order = [place ^ 3, place ^ 1, place ^ 2, place]
    arrived = [jnp.where(index // 2 == side, 2 + index % 2, index % 2) for index in order]

    def owned_blocks(which, common):
        rest = (blocks - 2 - common) // 2
        return [which] + [2 + common + which * rest + i for i in range(rest)]

    common = 4
    attn_mine = owned_blocks(side, common)
    attn_theirs = owned_blocks(1 - side, common)
    qkv_mine = owned_blocks(side, 0)
    qkv_theirs = owned_blocks(1 - side, 0)
    first = 4

    shared = [2 + i for i in range(common)]
    core = lax.axis_index("tensor")

    lists = ([core], order, arrived, shared, attn_mine, [side] + attn_theirs, qkv_mine, [side] + qkv_theirs)
    at_core, at_order, at_arrived, at_shared, at_attn, at_attn_theirs, at_qkv, at_qkv_theirs = (
        sum(len(entries) for entries in lists[:index]) for index in range(len(lists))
    )
    plan = jnp.stack([jnp.asarray(entry, jnp.int32) for entries in lists for entry in entries])

    ids = step_ids.reshape(1, token_count)
    table = modulation.reshape(2 * modulation.shape[0], width)

    attn_rows = turn(plan, attn_out, at_order)
    attn = attn_out
    attn_far = lax.ppermute(attn, "tensor", core_swap)
    attn_pair = lax.ppermute(pick(plan, attn, at_attn_theirs, 1 + len(attn_theirs)), "dp", swap(dp))

    def qkv_input():
        values, _ = lax.optimization_barrier((hidden, sent1_gate[0]))
        moments = lax.psum(stats(values), "tensor")
        return modulate(plan, at_core, ids, moments, values, table, width)

    def qkv_ready(mod):
        store["mod"] = mod
        store["pieces"] = {}
        store["far_pieces"] = {}
        for index in range(len(PIECES)):
            if index:
                mod, _ = lax.optimization_barrier((mod, message))
            message = pick(plan, mod, at_qkv_theirs + sum(PIECES[:index]), PIECES[index])
            store["pieces"][index] = lax.ppermute(message, "dp", swap(dp))
        store["mod_far"] = lax.ppermute(store["mod"], "tensor", core_swap)
        store["rows"] = turn(plan, store["mod"], at_order)

    sent1_gate = []
    hooks = {0: (qkv_input, qkv_ready)}

    count = len(attn_mine)
    pair_sizes = (PIECES[0] - 1,) + PIECES[1:]

    def stage(k):
        needed = []
        for kind, far, first, size in CHUNKS[k]:
            if kind == "shared":
                needed.append(attn_far if far else attn)
            elif kind == "attn":
                needed.append(fetched("attn", far, 0))
            else:
                needed.append([fetched("qkv", far, index) for index, _, _ in qkv_pieces(first, size)])
        return needed

    def fetched(kind, far, index):
        if kind == "attn":
            near = attn_pair
        else:
            near = store["pieces"][index]
        if not far:
            return near
        key = (kind, index)
        if key not in store:
            store[key] = lax.ppermute(store.get(("near",) + key, near), "tensor", core_swap)
        return store[key]

    def landed(kind, far, index, value):
        if not far and ("near", kind, index) not in store:
            store["near", kind, index] = value
            store[kind, index] = lax.ppermute(value, "tensor", core_swap)
            if index == 0:
                store["other_" + kind] = turn(plan, value, at_arrived)

    def qkv_pieces(first, size):
        held = []
        for index, length in enumerate(pair_sizes):
            start = sum(pair_sizes[:index])
            low, high = max(first, start), min(first + size, start + length)
            if low < high:
                held.append((index, low - start, high - low))
        return held

    def make_part(k, raw):
        columns, others = [], []
        rows, other_rows = attn_rows, None
        for (kind, far, first, size), held in zip(CHUNKS[k], raw):
            if kind == "shared":
                columns.append((held, at_shared + first, size))
            elif kind == "attn":
                landed("attn", far, 0, held)
                columns.append((attn_far if far else attn, at_attn + first, size))
                others.append((held, 1 + first, size))
                other_rows = store["other_attn"]
            else:
                for (index, _, _), piece in zip(qkv_pieces(first, size), held):
                    landed("qkv", far, index, piece)
                rows, other_rows = store["rows"], store["other_qkv"]
                columns.append((store["mod_far" if far else "mod"], at_qkv + first, size))
                for (index, start, length), piece in zip(qkv_pieces(first, size), held):
                    others.append((piece, start + (1 if index == 0 else 0), length))
        result = gram(plan, rows, columns, other_rows, others)
        if k == GATE:
            sent1_gate.append(result[1])
        return result

    done = {}
    results = {}

    def finish(k, own, came):
        values = unpacked(came)
        at = 0
        for kind, far, first, size in CHUNKS[k]:
            end = at + size * LANES
            done[kind, far, first] = (own[:, at:end], values[:, at:end])
            at = end
        if "out" not in results and len([key for key in done if key[0] != "qkv"]) == 4:
            keys = [("shared", False, 0), ("shared", True, 0), ("attn", False, 0), ("attn", True, 0)]
            results["out"] = assemble([done[key] for key in keys], True, factor)

    pipeline(len(CHUNKS), make_part, stage, hooks, LATER, finish)
    sides = []
    for far in (False, True):
        parts = [done[key] for key in sorted(key for key in done if key[0] == "qkv" and key[1] == far)]
        sides.append(tuple(jnp.concatenate(pieces, axis=1) for pieces in zip(*parts)))
    qkv_rows = assemble(sides, False, factor)
    return (qkv_rows, results["out"])


def solution(mesh):
    lined = mesh.shape["dp"] == 8 and mesh.shape["tensor"] == 2
    return jax.shard_map(
        body if lined else plain_body,
        mesh=mesh,
        in_specs=(
            P(("groups", "dp"), "tensor"),
            P(("groups", "dp"), "tensor"),
            P(("groups", "dp")),
            P("groups", None, None),
        ),
        out_specs=(P(("groups", "dp", "tensor"), None), P(("groups", "dp", "tensor"), None)),
        check_vma=False,
    )
```

```python
import functools

import jax
import jax.numpy as jnp
from jax import lax
from jax.experimental import pallas as pl
from jax.experimental.pallas import tpu as pltpu
from jax.sharding import PartitionSpec as P

ROW_DEV = 512
LANES = 256


epsilon = 1e-06
VMEM = 16 << 20
TAIL = 16
LAG = 1
FIRST = False
DOUBLES = (0,)
COMMON = 4
PAIR = 2
ROWS_AT = 1
PICK_LATE = False
EARLY = False
LATER = (2, 3, 4, 5, 6, 7)
LAST = 8
GATE = 1
CHUNKS = [[("shared", False, 0, 4)], [("shared", True, 0, 4)], [("attn", False, 0, 4)], [("attn", True, 0, 4)], [("qkv", False, 0, 4)], [("qkv", True, 0, 4)], [("qkv", False, 4, 2)], [("qkv", True, 4, 2)]]
PIECES = (5, 2)


def lookup_table(step_ids, table):
    steps = table.shape[0]
    columns = table.shape[2]
    onehot = (step_ids[:, None] == jnp.arange(steps, dtype=jnp.int32)[None, :]).astype(jnp.float32)
    looked = jnp.dot(onehot, table.reshape(steps, 2 * columns), precision=lax.Precision.HIGHEST)
    return (looked[:, :columns], looked[:, columns:])


def gram_rows(window, full):
    return lax.dot_general(
        window, full, (((0,), (0,)), ((), ())), preferred_element_type=jnp.float32
    )


def plain_body(hidden, attn_out, step_ids, modulation):
    token_count = hidden.shape[0]
    local_width = hidden.shape[1]
    parts_tp = lax.axis_size("tensor")
    parts_dp = lax.axis_size("dp")
    width = local_width * parts_tp
    rows_dev = ROW_DEV
    factor = 2.0 / (token_count * parts_dp)
    column_start = lax.axis_index("tensor") * local_width
    local_table = lax.dynamic_slice_in_dim(modulation, column_start, local_width, 2)
    scale, shift = lookup_table(step_ids, local_table)
    values = hidden.astype(jnp.float32)
    moments = lax.psum((jnp.sum(values, axis=1), jnp.sum(values * values, axis=1)), "tensor")
    mean = (moments[0] / width)[:, None]
    meansq = (moments[1] / width)[:, None]
    normed = (values - mean) * lax.rsqrt(meansq - mean * mean + epsilon)
    local_mod = (normed * (1.0 + scale) + shift).astype(jnp.bfloat16)
    full_mod, full_attn = (
        lax.all_gather(local_mod, "tensor", axis=1, tiled=True),
        lax.all_gather(attn_out, "tensor", axis=1, tiled=True),
    )
    part_qkv = gram_rows(local_mod[:, :rows_dev], full_mod)
    part_out = gram_rows(attn_out[:, :rows_dev], full_attn)
    summed_qkv, summed_out = (
        lax.psum_scatter(part_qkv, "dp", scatter_dimension=0, tiled=True),
        lax.psum_scatter(part_out, "dp", scatter_dimension=0, tiled=True),
    )
    return (summed_qkv * factor, summed_out * factor)


def swap(size, mask=1):
    return [(i, i ^ mask) for i in range(size)]


def cut(values, start, size, axis):
    return lax.dynamic_slice_in_dim(values, start, size, axis)


FREE = pl.CostEstimate(flops=0, bytes_accessed=0, transcendentals=0)


def gridded(kernel, indices, grid, in_specs, out_specs, out_shape, *operands):
    return pl.pallas_call(
        kernel,
        grid_spec=pltpu.PrefetchScalarGridSpec(
            num_scalar_prefetch=1, grid=(grid,), in_specs=in_specs, out_specs=out_specs
        ),
        out_shape=out_shape,
        cost_estimate=FREE,
        compiler_params=pltpu.CompilerParams(vmem_limit_bytes=VMEM),
    )(indices, *operands)


def pick_kernel(at, source, out):
    out[...] = source[...]


def pick(plan, source, first, count):
    tokens = source.shape[0]
    return gridded(
        pick_kernel,
        plan,
        count,
        [pl.BlockSpec((tokens, LANES), lambda i, at: (0, at[first + i]))],
        pl.BlockSpec((tokens, LANES), lambda i, at: (0, i)),
        jax.ShapeDtypeStruct((tokens, LANES * count), source.dtype),
        source,
    )


def turn_kernel(at, source, out):
    out[...] = source[...].T


def turn(plan, source, first):
    tokens = source.shape[0]
    size = ROW_DEV // 4
    return gridded(
        turn_kernel,
        plan,
        4,
        [pl.BlockSpec((tokens, size), lambda i, at: (0, at[first + i]))],
        pl.BlockSpec((size, tokens), lambda i, at: (i, 0)),
        jax.ShapeDtypeStruct((ROW_DEV, tokens), source.dtype),
        source,
    )


def store_coded(total, message):
    rows = total.shape[0]
    peak = jnp.max(jnp.abs(total), axis=0, keepdims=True)
    power = jnp.ceil(jnp.log2(jnp.maximum(peak, 1e-30))) - 15.0
    codes = jnp.clip(jnp.round(total * jnp.exp2(-power)), -32767.0, 32767.0)
    message[:rows, :] = codes.astype(jnp.int32).astype(jnp.int16)
    tail = jnp.broadcast_to(power, (TAIL, total.shape[1]))
    message[rows:, :] = tail.astype(jnp.int32).astype(jnp.int16)


def decoded(message, first, last):
    power = message[message.shape[0] - TAIL :, :].astype(jnp.int32).astype(jnp.float32)[:1]
    return message[first:last, :].astype(jnp.int32).astype(jnp.float32) * jnp.exp2(power)


def chosen_piece(step, starts, pieces):
    sides = []
    for lane in range(PAIR):
        values = pieces[lane][...]
        for index, start in enumerate(starts[1:], 1):
            values = jnp.where(step < start, values, pieces[index * PAIR + lane][...])
        sides.append(values)
    return jnp.concatenate(sides, axis=1) if PAIR > 1 else sides[0]


def gram_kernel(starts, at, rows, *refs):
    own, message = refs[-2:]
    step = pl.program_id(0)
    mine = len(starts[0]) * PAIR
    total = jnp.dot(rows[...], chosen_piece(step, starts[0], refs[:mine]), preferred_element_type=jnp.float32)
    if starts[1]:
        columns = chosen_piece(step, starts[1], refs[mine + 1 : -2])
        total = total + jnp.dot(refs[mine][...], columns, preferred_element_type=jnp.float32)
    sent = message.shape[0] - TAIL
    own[...] = total[sent:]
    store_coded(total[:sent], message)


def gram(plan, rows, columns, other_rows=None, other_columns=()):
    tokens = rows.shape[1]
    whole = pl.BlockSpec((ROW_DEV, tokens), lambda i, at: (0, 0))
    in_specs, operands = [whole], [rows]
    starts = ([], [])
    for group, pieces in enumerate((columns, other_columns)):
        if group == 1 and pieces:
            in_specs.append(whole)
            operands.append(other_rows)
        start = 0
        for array, base, held in pieces:
            for lane in range(PAIR):

                def place(i, at, listed=group == 0, base=base, held=held, start=start, lane=lane):
                    index = jnp.clip(i - start, 0, held // PAIR - 1) * PAIR + lane + base
                    return (0, at[index] if listed else index)

                in_specs.append(pl.BlockSpec((tokens, LANES), place))
                operands.append(array)
            starts[group].append(start)
            start += held // PAIR
    count = sum(held for _, _, held in columns)
    width = LANES * count
    own = ROW_DEV // 2
    sent = ROW_DEV - own + TAIL
    size = LANES * PAIR
    return gridded(
        functools.partial(gram_kernel, tuple(map(tuple, starts))),
        plan,
        count // PAIR,
        in_specs,
        [pl.BlockSpec((own, size), lambda i, at: (0, i)), pl.BlockSpec((sent, size), lambda i, at: (0, i))],
        [jax.ShapeDtypeStruct((own, width), jnp.float32), jax.ShapeDtypeStruct((sent, width), jnp.int16)],
        *operands,
    )


def blocked(kernel, width, inputs, outputs):
    size = min(width, 2 * LANES)
    return pl.pallas_call(
        kernel,
        grid=(width // size,),
        in_specs=[pl.BlockSpec((rows, size), lambda i, at=at: (at, i)) for _, rows, at in inputs],
        out_specs=[pl.BlockSpec((rows, size), lambda i: (0, i)) for rows, _ in outputs],
        out_shape=[jax.ShapeDtypeStruct((rows, width), dtype) for rows, dtype in outputs],
        cost_estimate=FREE,
        compiler_params=pltpu.CompilerParams(vmem_limit_bytes=VMEM),
    )(*[array for array, _, _ in inputs])


def add_kernel(own, came, message):
    rows = own.shape[0]
    store_coded(own[...] + decoded(came, 0, rows), message)


def add_sums(own, came):
    rows = own.shape[0] // 2
    inputs = [(own, rows, 0), (came, came.shape[0], 0)]
    return blocked(add_kernel, own.shape[1], inputs, [(rows + TAIL, jnp.int16)])[0]


def total_kernel(own, came1, came2, mine, message):
    rows = own.shape[0]
    total = own[...] + decoded(came1, rows, 2 * rows) + decoded(came2, 0, rows)
    side = lax.rem(lax.axis_index("dp"), 2)
    half = rows // 2
    low, high = total[:half], total[half:]
    mine[...] = jnp.where(side == 0, low, high)
    store_coded(jnp.where(side == 0, high, low), message)


def total_sums(own, came1, came2):
    rows = own.shape[0] // 2
    inputs = [(own, rows, 1), (came1, came1.shape[0], 0), (came2, came2.shape[0], 0)]
    outputs = [(rows // 2, jnp.float32), (rows // 2 + TAIL, jnp.int16)]
    return blocked(total_kernel, own.shape[1], inputs, outputs)


def token_columns(rows):
    full = jnp.concatenate([rows, jnp.zeros((8 - rows.shape[0], rows.shape[1]), rows.dtype)], axis=0)
    return full.T


def chosen_rows(ids, steps, kind, repeat):
    place = lax.broadcasted_iota(jnp.int32, (ids.shape[0], repeat * 2 * steps), 1)
    return (2.0 * ids + kind).astype(jnp.int32) == lax.rem(place, 2 * steps)


def stats_kernel(hidden, moments):
    values = hidden[...].astype(jnp.float32)
    total = jnp.sum(values, axis=1, keepdims=True)
    squares = jnp.sum(values * values, axis=1, keepdims=True)
    lane = lax.broadcasted_iota(jnp.int32, (values.shape[0], 128), 1)
    moments[...] = jnp.where(lane == 0, total, jnp.where(lane == 1, squares, 0.0)).T[:8]


def stats(hidden):
    tokens, width = hidden.shape
    size = tokens // 4
    return pl.pallas_call(
        stats_kernel,
        grid=(4,),
        in_specs=[pl.BlockSpec((size, width), lambda i: (i, 0))],
        out_specs=pl.BlockSpec((8, size), lambda i: (0, i)),
        out_shape=jax.ShapeDtypeStruct((8, tokens), jnp.float32),
        cost_estimate=FREE,
        compiler_params=pltpu.CompilerParams(vmem_limit_bytes=VMEM),
    )(hidden)


def modulate_kernel(width, at, ids, moments, values, table, out):
    steps = table.shape[0] // 2
    turned = token_columns(jnp.concatenate([moments[...][:2], ids[...].astype(jnp.float32)], axis=0))
    mean = turned[:, :1] * (1.0 / width)
    meansq = turned[:, 1:2] * (1.0 / width)
    gain = lax.rsqrt(meansq - mean * mean + epsilon)
    entries = table[...]
    pieces = []
    for _ in range(3):
        piece = entries.astype(jnp.bfloat16).astype(jnp.float32)
        entries = entries - piece
        pieces.append(piece)
    split = jnp.concatenate(pieces, axis=0).astype(jnp.bfloat16)

    def lookup(kind):
        onehot = chosen_rows(turned[:, 2:3], steps, kind, 3).astype(jnp.bfloat16)
        return jnp.dot(onehot, split, preferred_element_type=jnp.float32)

    normed = (values[...].astype(jnp.float32) - mean) * gain
    out[...] = (normed * (1.0 + lookup(0)) + lookup(1)).astype(jnp.bfloat16)


def modulate(plan, at_core, step_ids, moments, values, table, width):
    tokens, local_width = values.shape
    size = 2 * LANES
    count = local_width // size
    columns = pl.BlockSpec((tokens, size), lambda i, at: (0, i))
    return gridded(
        functools.partial(modulate_kernel, width),
        plan,
        count,
        [
            pl.BlockSpec((1, tokens), lambda i, at: (0, 0)),
            pl.BlockSpec((8, tokens), lambda i, at: (0, 0)),
            columns,
            pl.BlockSpec((table.shape[0], size), lambda i, at: (0, at[at_core] * count + i)),
        ],
        columns,
        jax.ShapeDtypeStruct(values.shape, jnp.bfloat16),
        step_ids,
        moments,
        values,
        table,
    )


def pipeline(count, make_part, stage, hooks, extras, later, finish):
    own, sent1, came1, came2, came3, owned = {}, {}, {}, {}, {}, {}
    due2, due3 = {}, {}
    for j in range(count):
        due2[j] = max(j + 1, min(j + (LAG if j < LAST else 1), count))
        due3[j] = due2[j] + 1

    def begin(k, raw):
        own[k], sent1[k] = make_part(k, raw)
        came1[k] = lax.ppermute(sent1[k], "dp", swap(8, 2))

    begin(0, stage(0))
    if GATE:
        begin(1, stage(1))
    else:
        ready, raw = lax.optimization_barrier((hooks[0][0](), stage(1)))
        hooks = {0: (lambda: ready, hooks[0][1])}
        begin(1, raw)
    for k in range(max(due3.values()) + 1):
        now2 = [j for j in range(count) if due2[j] == k]
        now3 = [j for j in range(count) if due3[j] == k]
        wanted = {}
        if k < count:
            wanted["came1"] = came1[k]
        if k + 1 < count:
            wanted["sent1"] = sent1[k + 1]
        if k in hooks:
            wanted["more"] = hooks[k][0]()
        if k in extras:
            wanted["extra"] = extras[k][0]()
        if k in DOUBLES:
            wanted["next1"] = came1[k + 1]
        wanted = lax.optimization_barrier(wanted)
        if k in hooks:
            hooks[k][1](wanted["more"])
        if k in extras:
            extras[k][1](wanted["extra"])
        if k in DOUBLES:
            came1[k + 1] = wanted["next1"]
        if k + 2 < count and k + 2 not in later:
            raw, _ = lax.optimization_barrier((stage(k + 2), wanted["came1"]))
            begin(k + 2, raw)
            wanted, _ = lax.optimization_barrier((wanted, sent1[k + 2]))
        ahead = []
        if k < count:
            came1[k] = wanted["came1"]
            sent = add_sums(own[k], came1[k])
            ahead.append(sent)
            came2[k] = lax.ppermute(sent, "dp", swap(8, 4))
        rest = {"came2": [came2[j] for j in now2]}
        rest, _ = lax.optimization_barrier((rest, wanted["came1"] if FIRST and k < count else ahead))
        if EARLY and k + 2 < count and k + 2 in later:
            raw, _ = lax.optimization_barrier((stage(k + 2), tuple(ahead)))
            begin(k + 2, raw)
            rest, _ = lax.optimization_barrier((rest, sent1[k + 2]))
        for j, came in zip(now2, rest["came2"]):
            owned[j], sent = total_sums(own[j], came1[j], came)
            ahead.append(sent)
            came3[j] = lax.ppermute(sent, "dp", swap(8))
        ended, _ = lax.optimization_barrier(([came3[j] for j in now3], tuple(ahead)))
        for j, came in zip(now3, ended):
            finish(j, owned[j], came)
        if not EARLY and k + 2 < count and k + 2 in later:
            raw, _ = lax.optimization_barrier((stage(k + 2), tuple(ahead)))
            begin(k + 2, raw)


def unpacked(message):
    rows = message.shape[0] - TAIL
    return message[:rows].astype(jnp.float32) * jnp.exp2(message[rows : rows + 1].astype(jnp.float32))


def in_order(own, other):
    side = lax.axis_index("dp") % 2
    return jnp.where(side == 0, own, other), jnp.where(side == 0, other, own)


def assemble(done, shared, scale):
    core = lax.axis_index("tensor")
    half = ROW_DEV // 2
    cores = []
    for which in range(2):
        mine = done[which::2]
        pieces = []
        if shared:
            pieces.append(mine[0][0] + mine[0][1])
            mine = mine[1:]
        ordered = [in_order(*pair) for pair in mine]
        head = [ordered[0][0][:, :half], ordered[0][1][:, :half]]
        ordered[0] = (ordered[0][0][:, half:], ordered[0][1][:, half:])
        pieces = head + pieces + [pair[0] for pair in ordered] + [pair[1] for pair in ordered]
        cores.append(jnp.concatenate(pieces, axis=1))
    left = jnp.where(core == 0, cores[0], cores[1])
    right = jnp.where(core == 0, cores[1], cores[0])
    return jnp.concatenate([left, right], axis=1) * scale


def body(hidden, attn_out, step_ids, modulation):
    token_count = hidden.shape[0]
    local_width = hidden.shape[1]
    parts_tp = lax.axis_size("tensor")
    dp = lax.axis_size("dp")
    width = local_width * parts_tp
    tokens = token_count * dp
    factor = 2.0 / tokens
    core_swap = swap(2)
    side = lax.axis_index("dp") % 2
    place = lax.axis_index("dp") // 2
    blocks = local_width // LANES
    store = {}

    order = [place ^ 3, place ^ 1, place ^ 2, place]
    arrived = [jnp.where(index // 2 == side, 2 + index % 2, index % 2) for index in order]

    def owned_blocks(which, common):
        rest = (blocks - 2 - common) // 2
        return [which] + [2 + common + which * rest + i for i in range(rest)]

    common = COMMON
    attn_mine = owned_blocks(side, common)
    attn_theirs = owned_blocks(1 - side, common)
    qkv_mine = owned_blocks(side, 0)
    qkv_theirs = owned_blocks(1 - side, 0)
    first = 4

    shared = [2 + i for i in range(common)]
    core = lax.axis_index("tensor")

    lists = ([core], order, arrived, shared, attn_mine, [side] + attn_theirs, qkv_mine, [side] + qkv_theirs)
    at_core, at_order, at_arrived, at_shared, at_attn, at_attn_theirs, at_qkv, at_qkv_theirs = (
        sum(len(entries) for entries in lists[:index]) for index in range(len(lists))
    )
    plan = jnp.stack([jnp.asarray(entry, jnp.int32) for entries in lists for entry in entries])

    ids = step_ids.reshape(1, token_count)
    table = modulation.reshape(2 * modulation.shape[0], width)

    attn_rows = turn(plan, attn_out, at_order)
    attn = attn_out
    attn_far = lax.ppermute(attn, "tensor", core_swap)
    if not PICK_LATE:
        store["attn_pair"] = lax.ppermute(pick(plan, attn, at_attn_theirs, 1 + len(attn_theirs)), "dp", swap(dp))

    def qkv_input():
        values, _ = lax.optimization_barrier((hidden, sent1_gate[0]))
        moments = lax.psum(stats(values), "tensor")
        return modulate(plan, at_core, ids, moments, values, table, width)

    def qkv_ready(mod):
        store["mod"] = mod
        store["pieces"] = {}
        store["far_pieces"] = {}
        for index in range(len(PIECES)):
            if index:
                mod, _ = lax.optimization_barrier((mod, message))
            message = pick(plan, mod, at_qkv_theirs + sum(PIECES[:index]), PIECES[index])
            store["pieces"][index] = lax.ppermute(message, "dp", swap(dp))
        store["mod_far"] = lax.ppermute(store["mod"], "tensor", core_swap)
        store["rows"] = turn(plan, store["mod"], at_order)

    sent1_gate = []
    extras = {}
    if ROWS_AT:
        extras[ROWS_AT] = (lambda: store["rows"], lambda value: store.update(rows=value))
    hooks = {0: (qkv_input, qkv_ready)}

    count = len(attn_mine)
    pair_sizes = (PIECES[0] - 1,) + PIECES[1:]

    def stage(k):
        needed = []
        for kind, far, first, size in CHUNKS[k]:
            if kind == "shared":
                needed.append(attn_far if far else attn)
            elif kind == "attn":
                needed.append(fetched("attn", far, 0))
            else:
                needed.append([fetched("qkv", far, index) for index, _, _ in qkv_pieces(first, size)])
        return needed

    def fetched(kind, far, index):
        if kind == "attn":
            near = store["attn_pair"]
        else:
            near = store["pieces"][index]
        if not far:
            return near
        key = (kind, index)
        if key not in store:
            store[key] = lax.ppermute(store.get(("near",) + key, near), "tensor", core_swap)
        return store[key]

    def landed(kind, far, index, value):
        if not far and ("near", kind, index) not in store:
            store["near", kind, index] = value
            store[kind, index] = lax.ppermute(value, "tensor", core_swap)
            if index == 0:
                store["other_" + kind] = turn(plan, value, at_arrived)

    def qkv_pieces(first, size):
        held = []
        for index, length in enumerate(pair_sizes):
            start = sum(pair_sizes[:index])
            low, high = max(first, start), min(first + size, start + length)
            if low < high:
                held.append((index, low - start, high - low))
        return held

    def make_part(k, raw):
        columns, others = [], []
        rows, other_rows = attn_rows, None
        for (kind, far, first, size), held in zip(CHUNKS[k], raw):
            if kind == "shared":
                columns.append((held, at_shared + first, size))
            elif kind == "attn":
                landed("attn", far, 0, held)
                columns.append((attn_far if far else attn, at_attn + first, size))
                others.append((held, 1 + first, size))
                other_rows = store["other_attn"]
            else:
                for (index, _, _), piece in zip(qkv_pieces(first, size), held):
                    landed("qkv", far, index, piece)
                rows, other_rows = store["rows"], store["other_qkv"]
                columns.append((store["mod_far" if far else "mod"], at_qkv + first, size))
                for (index, start, length), piece in zip(qkv_pieces(first, size), held):
                    others.append((piece, start + (1 if index == 0 else 0), length))
        result = gram(plan, rows, columns, other_rows, others)
        if k == 0 and PICK_LATE:
            late, _ = lax.optimization_barrier((attn, result[1]))
            store["attn_pair"] = lax.ppermute(pick(plan, late, at_attn_theirs, 1 + len(attn_theirs)), "dp", swap(dp))
        if k == GATE:
            sent1_gate.append(result[1])
        return result

    done = {}
    results = {}

    def finish(k, own, came):
        values = unpacked(came)
        at = 0
        for kind, far, first, size in CHUNKS[k]:
            end = at + size * LANES
            done[kind, far, first] = (own[:, at:end], values[:, at:end])
            at = end
        kinds = [entry[0] for parts in CHUNKS for entry in parts if entry[0] != "qkv"]
        if "out" not in results and len([key for key in done if key[0] != "qkv"]) == len(kinds):
            joined = [gathered(kind, far) for kind in ("shared", "attn") for far in (False, True)]
            results["out"] = assemble(joined, True, factor)

    def gathered(kind, far):
        parts = [done[key] for key in sorted(key for key in done if key[:2] == (kind, far))]
        return tuple(jnp.concatenate(pieces, axis=1) for pieces in zip(*parts))

    pipeline(len(CHUNKS), make_part, stage, hooks, extras, LATER, finish)
    qkv_rows = assemble([gathered("qkv", far) for far in (False, True)], False, factor)
    return (qkv_rows, results["out"])


def solution(mesh):
    lined = mesh.shape["dp"] == 8 and mesh.shape["tensor"] == 2
    return jax.shard_map(
        body if lined else plain_body,
        mesh=mesh,
        in_specs=(
            P(("groups", "dp"), "tensor"),
            P(("groups", "dp"), "tensor"),
            P(("groups", "dp")),
            P("groups", None, None),
        ),
        out_specs=(P(("groups", "dp", "tensor"), None), P(("groups", "dp", "tensor"), None)),
        check_vma=False,
    )
```

```python
import functools

import jax
import jax.numpy as jnp
from jax import lax
from jax.experimental import pallas as pl
from jax.experimental.pallas import tpu as pltpu
from jax.sharding import PartitionSpec as P

ROW_DEV = 512
LANES = 256


epsilon = 1e-06
VMEM = 16 << 20
TAIL = 8
LAG = 1
FIRST = False
DOUBLES = (0,)
COMMON = 4
HOOK_LATE = 2
PAIR = 2
ROWS_AT = 1
PICK_LATE = False
EARLY = False
LATER = (2, 3, 4, 5, 6, 7)
LAST = 8
GATE = 1
CHUNKS = [[("shared", False, 0, 4)], [("shared", True, 0, 4)], [("attn", False, 0, 4)], [("attn", True, 0, 4)], [("qkv", False, 0, 4)], [("qkv", True, 0, 4)], [("qkv", False, 4, 2)], [("qkv", True, 4, 2)]]
PIECES = (5, 2)


def lookup_table(step_ids, table):
    steps = table.shape[0]
    columns = table.shape[2]
    onehot = (step_ids[:, None] == jnp.arange(steps, dtype=jnp.int32)[None, :]).astype(jnp.float32)
    looked = jnp.dot(onehot, table.reshape(steps, 2 * columns), precision=lax.Precision.HIGHEST)
    return (looked[:, :columns], looked[:, columns:])


def gram_rows(window, full):
    return lax.dot_general(
        window, full, (((0,), (0,)), ((), ())), preferred_element_type=jnp.float32
    )


def plain_body(hidden, attn_out, step_ids, modulation):
    token_count = hidden.shape[0]
    local_width = hidden.shape[1]
    parts_tp = lax.axis_size("tensor")
    parts_dp = lax.axis_size("dp")
    width = local_width * parts_tp
    rows_dev = ROW_DEV
    factor = 2.0 / (token_count * parts_dp)
    column_start = lax.axis_index("tensor") * local_width
    local_table = lax.dynamic_slice_in_dim(modulation, column_start, local_width, 2)
    scale, shift = lookup_table(step_ids, local_table)
    values = hidden.astype(jnp.float32)
    moments = lax.psum((jnp.sum(values, axis=1), jnp.sum(values * values, axis=1)), "tensor")
    mean = (moments[0] / width)[:, None]
    meansq = (moments[1] / width)[:, None]
    normed = (values - mean) * lax.rsqrt(meansq - mean * mean + epsilon)
    local_mod = (normed * (1.0 + scale) + shift).astype(jnp.bfloat16)
    full_mod, full_attn = (
        lax.all_gather(local_mod, "tensor", axis=1, tiled=True),
        lax.all_gather(attn_out, "tensor", axis=1, tiled=True),
    )
    part_qkv = gram_rows(local_mod[:, :rows_dev], full_mod)
    part_out = gram_rows(attn_out[:, :rows_dev], full_attn)
    summed_qkv, summed_out = (
        lax.psum_scatter(part_qkv, "dp", scatter_dimension=0, tiled=True),
        lax.psum_scatter(part_out, "dp", scatter_dimension=0, tiled=True),
    )
    return (summed_qkv * factor, summed_out * factor)


def swap(size, mask=1):
    return [(i, i ^ mask) for i in range(size)]


def cut(values, start, size, axis):
    return lax.dynamic_slice_in_dim(values, start, size, axis)


FREE = pl.CostEstimate(flops=0, bytes_accessed=0, transcendentals=0)


def gridded(kernel, indices, grid, in_specs, out_specs, out_shape, *operands):
    return pl.pallas_call(
        kernel,
        grid_spec=pltpu.PrefetchScalarGridSpec(
            num_scalar_prefetch=1, grid=(grid,), in_specs=in_specs, out_specs=out_specs
        ),
        out_shape=out_shape,
        cost_estimate=FREE,
        compiler_params=pltpu.CompilerParams(vmem_limit_bytes=VMEM),
    )(indices, *operands)


def pick_kernel(first, runs, at, source, out, sems):
    copies = []
    start = 0
    for index, length in enumerate(runs):
        columns = pl.ds(pl.multiple_of(at[first + start] * LANES, LANES), length * LANES)
        copy = pltpu.make_async_copy(
            source.at[:, columns], out.at[:, start * LANES : (start + length) * LANES], sems.at[index]
        )
        copy.start()
        copies.append(copy)
        start += length
    for copy in copies:
        copy.wait()


def pick(plan, source, first, runs):
    return pl.pallas_call(
        functools.partial(pick_kernel, first, runs),
        grid_spec=pltpu.PrefetchScalarGridSpec(
            num_scalar_prefetch=1,
            grid=(1,),
            in_specs=[pl.BlockSpec(memory_space=pl.ANY)],
            out_specs=pl.BlockSpec(memory_space=pl.ANY),
            scratch_shapes=[pltpu.SemaphoreType.DMA((len(runs),))],
        ),
        out_shape=jax.ShapeDtypeStruct((source.shape[0], LANES * sum(runs)), source.dtype),
        cost_estimate=FREE,
        compiler_params=pltpu.CompilerParams(vmem_limit_bytes=VMEM),
    )(plan, source)


def turn_kernel(at, source, out):
    out[...] = source[...].T


def turn(plan, source, first):
    tokens = source.shape[0]
    size = ROW_DEV // 4
    return gridded(
        turn_kernel,
        plan,
        4,
        [pl.BlockSpec((tokens, size), lambda i, at: (0, at[first + i]))],
        pl.BlockSpec((size, tokens), lambda i, at: (i, 0)),
        jax.ShapeDtypeStruct((ROW_DEV, tokens), source.dtype),
        source,
    )


def store_coded(total, message):
    rows = total.shape[0]
    peak = jnp.max(jnp.abs(total), axis=0, keepdims=True)
    power = jnp.ceil(jnp.log2(jnp.maximum(peak, 1e-30))) - 15.0
    codes = jnp.clip(jnp.round(total * jnp.exp2(-power)), -32767.0, 32767.0)
    message[:rows, :] = codes.astype(jnp.int32).astype(jnp.int16)
    tail = jnp.broadcast_to(power, (TAIL, total.shape[1]))
    message[rows:, :] = tail.astype(jnp.int32).astype(jnp.int16)


def decoded(message, first, last):
    power = message[message.shape[0] - TAIL :, :].astype(jnp.int32).astype(jnp.float32)[:1]
    return message[first:last, :].astype(jnp.int32).astype(jnp.float32) * jnp.exp2(power)


def chosen_piece(step, starts, pieces):
    sides = []
    for lane in range(PAIR):
        values = pieces[lane][...]
        for index, start in enumerate(starts[1:], 1):
            values = jnp.where(step < start, values, pieces[index * PAIR + lane][...])
        sides.append(values)
    return jnp.concatenate(sides, axis=1) if PAIR > 1 else sides[0]


def gram_kernel(starts, at, rows, *refs):
    own, message = refs[-2:]
    step = pl.program_id(0)
    mine = len(starts[0]) * PAIR
    total = jnp.dot(rows[...], chosen_piece(step, starts[0], refs[:mine]), preferred_element_type=jnp.float32)
    if starts[1]:
        columns = chosen_piece(step, starts[1], refs[mine + 1 : -2])
        total = total + jnp.dot(refs[mine][...], columns, preferred_element_type=jnp.float32)
    sent = message.shape[0] - TAIL
    own[...] = total[sent:]
    store_coded(total[:sent], message)


def gram(plan, rows, columns, other_rows=None, other_columns=()):
    tokens = rows.shape[1]
    whole = pl.BlockSpec((ROW_DEV, tokens), lambda i, at: (0, 0))
    in_specs, operands = [whole], [rows]
    starts = ([], [])
    for group, pieces in enumerate((columns, other_columns)):
        if group == 1 and pieces:
            in_specs.append(whole)
            operands.append(other_rows)
        start = 0
        for array, base, held in pieces:
            for lane in range(PAIR):

                def place(i, at, listed=group == 0, base=base, held=held, start=start, lane=lane):
                    index = jnp.clip(i - start, 0, held // PAIR - 1) * PAIR + lane + base
                    return (0, at[index] if listed else index)

                in_specs.append(pl.BlockSpec((tokens, LANES), place))
                operands.append(array)
            starts[group].append(start)
            start += held // PAIR
    count = sum(held for _, _, held in columns)
    width = LANES * count
    own = ROW_DEV // 2
    sent = ROW_DEV - own + TAIL
    size = LANES * PAIR
    return gridded(
        functools.partial(gram_kernel, tuple(map(tuple, starts))),
        plan,
        count // PAIR,
        in_specs,
        [pl.BlockSpec((own, size), lambda i, at: (0, i)), pl.BlockSpec((sent, size), lambda i, at: (0, i))],
        [jax.ShapeDtypeStruct((own, width), jnp.float32), jax.ShapeDtypeStruct((sent, width), jnp.int16)],
        *operands,
    )


def blocked(kernel, width, inputs, outputs):
    size = min(width, 2 * LANES)
    return pl.pallas_call(
        kernel,
        grid=(width // size,),
        in_specs=[pl.BlockSpec((rows, size), lambda i, at=at: (at, i)) for _, rows, at in inputs],
        out_specs=[pl.BlockSpec((rows, size), lambda i: (0, i)) for rows, _ in outputs],
        out_shape=[jax.ShapeDtypeStruct((rows, width), dtype) for rows, dtype in outputs],
        cost_estimate=FREE,
        compiler_params=pltpu.CompilerParams(vmem_limit_bytes=VMEM),
    )(*[array for array, _, _ in inputs])


def add_kernel(own, came, message):
    rows = own.shape[0]
    store_coded(own[...] + decoded(came, 0, rows), message)


def add_sums(own, came):
    rows = own.shape[0] // 2
    inputs = [(own, rows, 0), (came, came.shape[0], 0)]
    return blocked(add_kernel, own.shape[1], inputs, [(rows + TAIL, jnp.int16)])[0]


def total_kernel(own, came1, came2, mine, message):
    rows = own.shape[0]
    total = own[...] + decoded(came1, rows, 2 * rows) + decoded(came2, 0, rows)
    side = lax.rem(lax.axis_index("dp"), 2)
    half = rows // 2
    low, high = total[:half], total[half:]
    mine[...] = jnp.where(side == 0, low, high)
    store_coded(jnp.where(side == 0, high, low), message)


def total_sums(own, came1, came2):
    rows = own.shape[0] // 2
    inputs = [(own, rows, 1), (came1, came1.shape[0], 0), (came2, came2.shape[0], 0)]
    outputs = [(rows // 2, jnp.float32), (rows // 2 + TAIL, jnp.int16)]
    return blocked(total_kernel, own.shape[1], inputs, outputs)


def token_columns(rows):
    full = jnp.concatenate([rows, jnp.zeros((8 - rows.shape[0], rows.shape[1]), rows.dtype)], axis=0)
    return full.T


def chosen_rows(ids, steps, kind, repeat):
    place = lax.broadcasted_iota(jnp.int32, (ids.shape[0], repeat * 2 * steps), 1)
    return (2.0 * ids + kind).astype(jnp.int32) == lax.rem(place, 2 * steps)


def stats_kernel(hidden, moments):
    values = hidden[...].astype(jnp.float32)
    total = jnp.sum(values, axis=1, keepdims=True)
    squares = jnp.sum(values * values, axis=1, keepdims=True)
    lane = lax.broadcasted_iota(jnp.int32, (values.shape[0], 128), 1)
    moments[...] = jnp.where(lane == 0, total, jnp.where(lane == 1, squares, 0.0)).T[:8]


def stats(hidden):
    tokens, width = hidden.shape
    size = tokens // 4
    return pl.pallas_call(
        stats_kernel,
        grid=(4,),
        in_specs=[pl.BlockSpec((size, width), lambda i: (i, 0))],
        out_specs=pl.BlockSpec((8, size), lambda i: (0, i)),
        out_shape=jax.ShapeDtypeStruct((8, tokens), jnp.float32),
        cost_estimate=FREE,
        compiler_params=pltpu.CompilerParams(vmem_limit_bytes=VMEM),
    )(hidden)


def modulate_kernel(width, at, ids, moments, values, table, out):
    steps = table.shape[0] // 2
    turned = token_columns(jnp.concatenate([moments[...][:2], ids[...].astype(jnp.float32)], axis=0))
    mean = turned[:, :1] * (1.0 / width)
    meansq = turned[:, 1:2] * (1.0 / width)
    gain = lax.rsqrt(meansq - mean * mean + epsilon)
    entries = table[...]
    pieces = []
    for _ in range(3):
        piece = entries.astype(jnp.bfloat16).astype(jnp.float32)
        entries = entries - piece
        pieces.append(piece)
    split = jnp.concatenate(pieces, axis=0).astype(jnp.bfloat16)

    def lookup(kind):
        onehot = chosen_rows(turned[:, 2:3], steps, kind, 3).astype(jnp.bfloat16)
        return jnp.dot(onehot, split, preferred_element_type=jnp.float32)

    normed = (values[...].astype(jnp.float32) - mean) * gain
    out[...] = (normed * (1.0 + lookup(0)) + lookup(1)).astype(jnp.bfloat16)


def modulate(plan, at_core, step_ids, moments, values, table, width):
    tokens, local_width = values.shape
    size = 2 * LANES
    count = local_width // size
    columns = pl.BlockSpec((tokens, size), lambda i, at: (0, i))
    return gridded(
        functools.partial(modulate_kernel, width),
        plan,
        count,
        [
            pl.BlockSpec((1, tokens), lambda i, at: (0, 0)),
            pl.BlockSpec((8, tokens), lambda i, at: (0, 0)),
            columns,
            pl.BlockSpec((table.shape[0], size), lambda i, at: (0, at[at_core] * count + i)),
        ],
        columns,
        jax.ShapeDtypeStruct(values.shape, jnp.bfloat16),
        step_ids,
        moments,
        values,
        table,
    )


def pipeline(count, make_part, stage, hooks, extras, later, finish):
    own, sent1, came1, came2, came3, owned = {}, {}, {}, {}, {}, {}
    due2, due3 = {}, {}
    for j in range(count):
        due2[j] = max(j + 1, min(j + (LAG if j < LAST else 1), count))
        due3[j] = due2[j] + 1

    def begin(k, raw):
        own[k], sent1[k] = make_part(k, raw)
        came1[k] = lax.ppermute(sent1[k], "dp", swap(8, 2))

    begin(0, stage(0))
    if GATE:
        begin(1, stage(1))
    else:
        ready, raw = lax.optimization_barrier((hooks[0][0](), stage(1)))
        hooks = {0: (lambda: ready, hooks[0][1])}
        begin(1, raw)
    for k in range(max(due3.values()) + 1):
        now2 = [j for j in range(count) if due2[j] == k]
        now3 = [j for j in range(count) if due3[j] == k]
        wanted = {}
        if k < count:
            wanted["came1"] = came1[k]
        if k + 1 < count:
            wanted["sent1"] = sent1[k + 1]
        if k in hooks:
            wanted["more"] = hooks[k][0]()
        if k in extras:
            wanted["extra"] = extras[k][0]()
        if k in DOUBLES:
            wanted["next1"] = came1[k + 1]
        wanted = lax.optimization_barrier(wanted)
        if k in hooks and not HOOK_LATE:
            hooks[k][1](wanted["more"])
        if k in extras:
            extras[k][1](wanted["extra"])
        if k in DOUBLES:
            came1[k + 1] = wanted["next1"]
        if k + 2 < count and k + 2 not in later:
            raw, _ = lax.optimization_barrier((stage(k + 2), wanted["came1"]))
            begin(k + 2, raw)
            wanted, _ = lax.optimization_barrier((wanted, sent1[k + 2]))
        ahead = []
        if k < count:
            came1[k] = wanted["came1"]
            sent = add_sums(own[k], came1[k])
            ahead.append(sent)
            came2[k] = lax.ppermute(sent, "dp", swap(8, 4))
        rest = {"came2": [came2[j] for j in now2]}
        rest, _ = lax.optimization_barrier((rest, wanted["came1"] if FIRST and k < count else ahead))
        if EARLY and k + 2 < count and k + 2 in later:
            raw, _ = lax.optimization_barrier((stage(k + 2), tuple(ahead)))
            begin(k + 2, raw)
            rest, _ = lax.optimization_barrier((rest, sent1[k + 2]))
        for j, came in zip(now2, rest["came2"]):
            owned[j], sent = total_sums(own[j], came1[j], came)
            ahead.append(sent)
            came3[j] = lax.ppermute(sent, "dp", swap(8))
        ended, _ = lax.optimization_barrier(([came3[j] for j in now3], tuple(ahead)))
        for j, came in zip(now3, ended):
            finish(j, owned[j], came)
        if not EARLY and k + 2 < count and k + 2 in later:
            raw, _ = lax.optimization_barrier((stage(k + 2), tuple(ahead)))
            begin(k + 2, raw)
        if k in hooks and HOOK_LATE:
            more, _ = lax.optimization_barrier((wanted["more"], sent1[k + 2] if HOOK_LATE == 1 else tuple(ahead)))
            hooks[k][1](more)


def unpacked(message):
    rows = message.shape[0] - TAIL
    return message[:rows].astype(jnp.float32) * jnp.exp2(message[rows : rows + 1].astype(jnp.float32))


def in_order(own, other):
    side = lax.axis_index("dp") % 2
    return jnp.where(side == 0, own, other), jnp.where(side == 0, other, own)


def assemble(done, shared, scale):
    core = lax.axis_index("tensor")
    half = ROW_DEV // 2
    cores = []
    for which in range(2):
        mine = done[which::2]
        pieces = []
        if shared:
            pieces.append(mine[0][0] + mine[0][1])
            mine = mine[1:]
        ordered = [in_order(*pair) for pair in mine]
        head = [ordered[0][0][:, :half], ordered[0][1][:, :half]]
        ordered[0] = (ordered[0][0][:, half:], ordered[0][1][:, half:])
        pieces = head + pieces + [pair[0] for pair in ordered] + [pair[1] for pair in ordered]
        cores.append(jnp.concatenate(pieces, axis=1))
    left = jnp.where(core == 0, cores[0], cores[1])
    right = jnp.where(core == 0, cores[1], cores[0])
    return jnp.concatenate([left, right], axis=1) * scale


def body(hidden, attn_out, step_ids, modulation):
    token_count = hidden.shape[0]
    local_width = hidden.shape[1]
    parts_tp = lax.axis_size("tensor")
    dp = lax.axis_size("dp")
    width = local_width * parts_tp
    tokens = token_count * dp
    factor = 2.0 / tokens
    core_swap = swap(2)
    side = lax.axis_index("dp") % 2
    place = lax.axis_index("dp") // 2
    blocks = local_width // LANES
    store = {}

    order = [place ^ 3, place ^ 1, place ^ 2, place]
    arrived = [jnp.where(index // 2 == side, 2 + index % 2, index % 2) for index in order]

    def owned_blocks(which, common):
        rest = (blocks - 2 - common) // 2
        return [which] + [2 + common + which * rest + i for i in range(rest)]

    common = COMMON
    attn_mine = owned_blocks(side, common)
    attn_theirs = owned_blocks(1 - side, common)
    qkv_mine = owned_blocks(side, 0)
    qkv_theirs = owned_blocks(1 - side, 0)
    first = 4

    shared = [2 + i for i in range(common)]
    core = lax.axis_index("tensor")

    lists = ([core], order, arrived, shared, attn_mine, [side] + attn_theirs, qkv_mine, [side] + qkv_theirs)
    at_core, at_order, at_arrived, at_shared, at_attn, at_attn_theirs, at_qkv, at_qkv_theirs = (
        sum(len(entries) for entries in lists[:index]) for index in range(len(lists))
    )
    plan = jnp.stack([jnp.asarray(entry, jnp.int32) for entries in lists for entry in entries])

    ids = step_ids.reshape(1, token_count)
    table = modulation.reshape(2 * modulation.shape[0], width)

    attn_rows = turn(plan, attn_out, at_order)
    attn = attn_out
    attn_far = lax.ppermute(attn, "tensor", core_swap)
    if not PICK_LATE:
        store["attn_pair"] = lax.ppermute(pick(plan, attn, at_attn_theirs, (1, 1, len(attn_theirs) - 1)), "dp", swap(dp))

    def qkv_input():
        values, _ = lax.optimization_barrier((hidden, sent1_gate[0]))
        moments = lax.psum(stats(values), "tensor")
        return modulate(plan, at_core, ids, moments, values, table, width)

    def qkv_ready(mod):
        store["mod"] = mod
        store["pieces"] = {}
        store["far_pieces"] = {}
        for index in range(len(PIECES)):
            if index:
                mod, _ = lax.optimization_barrier((mod, message))
            message = pick(plan, mod, at_qkv_theirs + sum(PIECES[:index]), (PIECES[index],) if index else (1, 1, PIECES[0] - 2))
            store["pieces"][index] = lax.ppermute(message, "dp", swap(dp))
        store["mod_far"] = lax.ppermute(store["mod"], "tensor", core_swap)
        store["rows"] = turn(plan, store["mod"], at_order)

    sent1_gate = []
    extras = {}
    if ROWS_AT:
        extras[ROWS_AT] = (lambda: store["rows"], lambda value: store.update(rows=value))
    hooks = {0: (qkv_input, qkv_ready)}

    count = len(attn_mine)
    pair_sizes = (PIECES[0] - 1,) + PIECES[1:]

    def stage(k):
        needed = []
        for kind, far, first, size in CHUNKS[k]:
            if kind == "shared":
                needed.append(attn_far if far else attn)
            elif kind == "attn":
                needed.append(fetched("attn", far, 0))
            else:
                needed.append([fetched("qkv", far, index) for index, _, _ in qkv_pieces(first, size)])
        return needed

    def fetched(kind, far, index):
        if kind == "attn":
            near = store["attn_pair"]
        else:
            near = store["pieces"][index]
        if not far:
            return near
        key = (kind, index)
        if key not in store:
            store[key] = lax.ppermute(store.get(("near",) + key, near), "tensor", core_swap)
        return store[key]

    def landed(kind, far, index, value):
        if not far and ("near", kind, index) not in store:
            store["near", kind, index] = value
            store[kind, index] = lax.ppermute(value, "tensor", core_swap)
            if index == 0:
                store["other_" + kind] = turn(plan, value, at_arrived)

    def qkv_pieces(first, size):
        held = []
        for index, length in enumerate(pair_sizes):
            start = sum(pair_sizes[:index])
            low, high = max(first, start), min(first + size, start + length)
            if low < high:
                held.append((index, low - start, high - low))
        return held

    def make_part(k, raw):
        columns, others = [], []
        rows, other_rows = attn_rows, None
        for (kind, far, first, size), held in zip(CHUNKS[k], raw):
            if kind == "shared":
                columns.append((held, at_shared + first, size))
            elif kind == "attn":
                landed("attn", far, 0, held)
                columns.append((attn_far if far else attn, at_attn + first, size))
                others.append((held, 1 + first, size))
                other_rows = store["other_attn"]
            else:
                for (index, _, _), piece in zip(qkv_pieces(first, size), held):
                    landed("qkv", far, index, piece)
                rows, other_rows = store["rows"], store["other_qkv"]
                columns.append((store["mod_far" if far else "mod"], at_qkv + first, size))
                for (index, start, length), piece in zip(qkv_pieces(first, size), held):
                    others.append((piece, start + (1 if index == 0 else 0), length))
        result = gram(plan, rows, columns, other_rows, others)
        if k == 0 and PICK_LATE:
            late, _ = lax.optimization_barrier((attn, result[1]))
            store["attn_pair"] = lax.ppermute(pick(plan, late, at_attn_theirs, (1, 1, len(attn_theirs) - 1)), "dp", swap(dp))
        if k == GATE:
            sent1_gate.append(result[1])
        return result

    done = {}
    results = {}

    def finish(k, own, came):
        values = unpacked(came)
        at = 0
        for kind, far, first, size in CHUNKS[k]:
            end = at + size * LANES
            done[kind, far, first] = (own[:, at:end], values[:, at:end])
            at = end
        kinds = [entry[0] for parts in CHUNKS for entry in parts if entry[0] != "qkv"]
        if "out" not in results and len([key for key in done if key[0] != "qkv"]) == len(kinds):
            joined = [gathered(kind, far) for kind in ("shared", "attn") for far in (False, True)]
            results["out"] = assemble(joined, True, factor)

    def gathered(kind, far):
        parts = [done[key] for key in sorted(key for key in done if key[:2] == (kind, far))]
        return tuple(jnp.concatenate(pieces, axis=1) for pieces in zip(*parts))

    pipeline(len(CHUNKS), make_part, stage, hooks, extras, LATER, finish)
    qkv_rows = assemble([gathered("qkv", far) for far in (False, True)], False, factor)
    return (qkv_rows, results["out"])


def solution(mesh):
    lined = mesh.shape["dp"] == 8 and mesh.shape["tensor"] == 2
    return jax.shard_map(
        body if lined else plain_body,
        mesh=mesh,
        in_specs=(
            P(("groups", "dp"), "tensor"),
            P(("groups", "dp"), "tensor"),
            P(("groups", "dp")),
            P("groups", None, None),
        ),
        out_specs=(P(("groups", "dp", "tensor"), None), P(("groups", "dp", "tensor"), None)),
        check_vma=False,
    )
```

```python
import functools

import jax
import jax.numpy as jnp
from jax import lax
from jax.experimental import pallas as pl
from jax.experimental.pallas import tpu as pltpu
from jax.sharding import PartitionSpec as P

ROW_DEV = 512
LANES = 256


epsilon = 1e-06
VMEM = 16 << 20
TAIL = 8
LAG = 1
FIRST = False
DOUBLES = (0,)
COMMON = 4
HOOK_LATE = 2
PAIR = 2
ROWS_AT = 1
PICK_LATE = False
EARLY = False
LATER = (2, 3, 4, 5, 6, 7)
LAST = 8
GATE = 1
CHUNKS = [[("shared", False, 0, 4)], [("shared", True, 0, 4)], [("attn", False, 0, 4)], [("attn", True, 0, 4)], [("qkv", False, 0, 4)], [("qkv", True, 0, 4)], [("qkv", False, 4, 2)], [("qkv", True, 4, 2)]]
PIECES = (5, 2)


def lookup_table(step_ids, table):
    steps = table.shape[0]
    columns = table.shape[2]
    onehot = (step_ids[:, None] == jnp.arange(steps, dtype=jnp.int32)[None, :]).astype(jnp.float32)
    looked = jnp.dot(onehot, table.reshape(steps, 2 * columns), precision=lax.Precision.HIGHEST)
    return (looked[:, :columns], looked[:, columns:])


def gram_rows(window, full):
    return lax.dot_general(
        window, full, (((0,), (0,)), ((), ())), preferred_element_type=jnp.float32
    )


def plain_body(hidden, attn_out, step_ids, modulation):
    token_count = hidden.shape[0]
    local_width = hidden.shape[1]
    parts_tp = lax.axis_size("tensor")
    parts_dp = lax.axis_size("dp")
    width = local_width * parts_tp
    rows_dev = ROW_DEV
    factor = 2.0 / (token_count * parts_dp)
    column_start = lax.axis_index("tensor") * local_width
    local_table = lax.dynamic_slice_in_dim(modulation, column_start, local_width, 2)
    scale, shift = lookup_table(step_ids, local_table)
    values = hidden.astype(jnp.float32)
    moments = lax.psum((jnp.sum(values, axis=1), jnp.sum(values * values, axis=1)), "tensor")
    mean = (moments[0] / width)[:, None]
    meansq = (moments[1] / width)[:, None]
    normed = (values - mean) * lax.rsqrt(meansq - mean * mean + epsilon)
    local_mod = (normed * (1.0 + scale) + shift).astype(jnp.bfloat16)
    full_mod, full_attn = (
        lax.all_gather(local_mod, "tensor", axis=1, tiled=True),
        lax.all_gather(attn_out, "tensor", axis=1, tiled=True),
    )
    part_qkv = gram_rows(local_mod[:, :rows_dev], full_mod)
    part_out = gram_rows(attn_out[:, :rows_dev], full_attn)
    summed_qkv, summed_out = (
        lax.psum_scatter(part_qkv, "dp", scatter_dimension=0, tiled=True),
        lax.psum_scatter(part_out, "dp", scatter_dimension=0, tiled=True),
    )
    return (summed_qkv * factor, summed_out * factor)


def swap(size, mask=1):
    return [(i, i ^ mask) for i in range(size)]


def cut(values, start, size, axis):
    return lax.dynamic_slice_in_dim(values, start, size, axis)


FREE = pl.CostEstimate(flops=0, bytes_accessed=0, transcendentals=0)


def gridded(kernel, indices, grid, in_specs, out_specs, out_shape, *operands):
    return pl.pallas_call(
        kernel,
        grid_spec=pltpu.PrefetchScalarGridSpec(
            num_scalar_prefetch=1, grid=(grid,), in_specs=in_specs, out_specs=out_specs
        ),
        out_shape=out_shape,
        cost_estimate=FREE,
        compiler_params=pltpu.CompilerParams(vmem_limit_bytes=VMEM),
    )(indices, *operands)


def pick_kernel(first, runs, at, source, out, sems):
    copies = []
    start = 0
    for index, length in enumerate(runs):
        columns = pl.ds(pl.multiple_of(at[first + start] * LANES, LANES), length * LANES)
        copy = pltpu.make_async_copy(
            source.at[:, columns], out.at[:, start * LANES : (start + length) * LANES], sems.at[index]
        )
        copy.start()
        copies.append(copy)
        start += length
    for copy in copies:
        copy.wait()


def pick(plan, source, first, runs):
    return pl.pallas_call(
        functools.partial(pick_kernel, first, runs),
        grid_spec=pltpu.PrefetchScalarGridSpec(
            num_scalar_prefetch=1,
            grid=(1,),
            in_specs=[pl.BlockSpec(memory_space=pl.ANY)],
            out_specs=pl.BlockSpec(memory_space=pl.ANY),
            scratch_shapes=[pltpu.SemaphoreType.DMA((len(runs),))],
        ),
        out_shape=jax.ShapeDtypeStruct((source.shape[0], LANES * sum(runs)), source.dtype),
        cost_estimate=FREE,
        compiler_params=pltpu.CompilerParams(vmem_limit_bytes=VMEM),
    )(plan, source)


def turn_kernel(first, at, source, out):
    size = out.shape[0] // 4
    for index in range(4):
        columns = pl.ds(pl.multiple_of(at[first + index] * size, size), size)
        out[index * size : (index + 1) * size, :] = source[:, columns].T


def turn(plan, source, first):
    tokens = source.shape[0]
    return gridded(
        functools.partial(turn_kernel, first),
        plan,
        1,
        [pl.BlockSpec((tokens, ROW_DEV), lambda i, at: (0, 0))],
        pl.BlockSpec((ROW_DEV, tokens), lambda i, at: (0, 0)),
        jax.ShapeDtypeStruct((ROW_DEV, tokens), source.dtype),
        source,
    )


def store_coded(total, message):
    rows = total.shape[0]
    peak = jnp.max(jnp.abs(total), axis=0, keepdims=True)
    power = jnp.ceil(jnp.log2(jnp.maximum(peak, 1e-30))) - 15.0
    codes = jnp.clip(jnp.round(total * jnp.exp2(-power)), -32767.0, 32767.0)
    message[:rows, :] = codes.astype(jnp.int32).astype(jnp.int16)
    tail = jnp.broadcast_to(power, (TAIL, total.shape[1]))
    message[rows:, :] = tail.astype(jnp.int32).astype(jnp.int16)


def decoded(message, first, last):
    power = message[message.shape[0] - TAIL :, :].astype(jnp.int32).astype(jnp.float32)[:1]
    return message[first:last, :].astype(jnp.int32).astype(jnp.float32) * jnp.exp2(power)


def chosen_piece(step, starts, pieces):
    sides = []
    for lane in range(PAIR):
        values = pieces[lane][...]
        for index, start in enumerate(starts[1:], 1):
            values = jnp.where(step < start, values, pieces[index * PAIR + lane][...])
        sides.append(values)
    return jnp.concatenate(sides, axis=1) if PAIR > 1 else sides[0]


def gram_kernel(starts, at, rows, *refs):
    own, message = refs[-2:]
    step = pl.program_id(0)
    mine = len(starts[0]) * PAIR
    total = jnp.dot(rows[...], chosen_piece(step, starts[0], refs[:mine]), preferred_element_type=jnp.float32)
    if starts[1]:
        columns = chosen_piece(step, starts[1], refs[mine + 1 : -2])
        total = total + jnp.dot(refs[mine][...], columns, preferred_element_type=jnp.float32)
    sent = message.shape[0] - TAIL
    own[...] = total[sent:]
    store_coded(total[:sent], message)


def gram(plan, rows, columns, other_rows=None, other_columns=()):
    tokens = rows.shape[1]
    whole = pl.BlockSpec((ROW_DEV, tokens), lambda i, at: (0, 0))
    in_specs, operands = [whole], [rows]
    starts = ([], [])
    for group, pieces in enumerate((columns, other_columns)):
        if group == 1 and pieces:
            in_specs.append(whole)
            operands.append(other_rows)
        start = 0
        for array, base, held in pieces:
            for lane in range(PAIR):

                def place(i, at, listed=group == 0, base=base, held=held, start=start, lane=lane):
                    index = jnp.clip(i - start, 0, held // PAIR - 1) * PAIR + lane + base
                    return (0, at[index] if listed else index)

                in_specs.append(pl.BlockSpec((tokens, LANES), place))
                operands.append(array)
            starts[group].append(start)
            start += held // PAIR
    count = sum(held for _, _, held in columns)
    width = LANES * count
    own = ROW_DEV // 2
    sent = ROW_DEV - own + TAIL
    size = LANES * PAIR
    return gridded(
        functools.partial(gram_kernel, tuple(map(tuple, starts))),
        plan,
        count // PAIR,
        in_specs,
        [pl.BlockSpec((own, size), lambda i, at: (0, i)), pl.BlockSpec((sent, size), lambda i, at: (0, i))],
        [jax.ShapeDtypeStruct((own, width), jnp.float32), jax.ShapeDtypeStruct((sent, width), jnp.int16)],
        *operands,
    )


def blocked(kernel, width, inputs, outputs):
    size = min(width, 2 * LANES)
    return pl.pallas_call(
        kernel,
        grid=(width // size,),
        in_specs=[pl.BlockSpec((rows, size), lambda i, at=at: (at, i)) for _, rows, at in inputs],
        out_specs=[pl.BlockSpec((rows, size), lambda i: (0, i)) for rows, _ in outputs],
        out_shape=[jax.ShapeDtypeStruct((rows, width), dtype) for rows, dtype in outputs],
        cost_estimate=FREE,
        compiler_params=pltpu.CompilerParams(vmem_limit_bytes=VMEM),
    )(*[array for array, _, _ in inputs])


def add_kernel(own, came, message):
    rows = own.shape[0]
    store_coded(own[...] + decoded(came, 0, rows), message)


def add_sums(own, came):
    rows = own.shape[0] // 2
    inputs = [(own, rows, 0), (came, came.shape[0], 0)]
    return blocked(add_kernel, own.shape[1], inputs, [(rows + TAIL, jnp.int16)])[0]


def total_kernel(own, came1, came2, mine, message):
    rows = own.shape[0]
    total = own[...] + decoded(came1, rows, 2 * rows) + decoded(came2, 0, rows)
    side = lax.rem(lax.axis_index("dp"), 2)
    half = rows // 2
    low, high = total[:half], total[half:]
    mine[...] = jnp.where(side == 0, low, high)
    store_coded(jnp.where(side == 0, high, low), message)


def total_sums(own, came1, came2):
    rows = own.shape[0] // 2
    inputs = [(own, rows, 1), (came1, came1.shape[0], 0), (came2, came2.shape[0], 0)]
    outputs = [(rows // 2, jnp.float32), (rows // 2 + TAIL, jnp.int16)]
    return blocked(total_kernel, own.shape[1], inputs, outputs)


def token_columns(rows):
    full = jnp.concatenate([rows, jnp.zeros((8 - rows.shape[0], rows.shape[1]), rows.dtype)], axis=0)
    return full.T


def chosen_rows(ids, steps, kind, repeat):
    place = lax.broadcasted_iota(jnp.int32, (ids.shape[0], repeat * 2 * steps), 1)
    return (2.0 * ids + kind).astype(jnp.int32) == lax.rem(place, 2 * steps)


def stats_kernel(hidden, moments):
    values = hidden[...].astype(jnp.float32)
    total = jnp.sum(values, axis=1, keepdims=True)
    squares = jnp.sum(values * values, axis=1, keepdims=True)
    lane = lax.broadcasted_iota(jnp.int32, (values.shape[0], 128), 1)
    moments[...] = jnp.where(lane == 0, total, jnp.where(lane == 1, squares, 0.0)).T[:8]


def stats(hidden):
    tokens, width = hidden.shape
    size = tokens // 4
    return pl.pallas_call(
        stats_kernel,
        grid=(4,),
        in_specs=[pl.BlockSpec((size, width), lambda i: (i, 0))],
        out_specs=pl.BlockSpec((8, size), lambda i: (0, i)),
        out_shape=jax.ShapeDtypeStruct((8, tokens), jnp.float32),
        cost_estimate=FREE,
        compiler_params=pltpu.CompilerParams(vmem_limit_bytes=VMEM),
    )(hidden)


def modulate_kernel(width, at, ids, moments, values, table, out):
    steps = table.shape[0] // 2
    turned = token_columns(jnp.concatenate([moments[...][:2], ids[...].astype(jnp.float32)], axis=0))
    mean = turned[:, :1] * (1.0 / width)
    meansq = turned[:, 1:2] * (1.0 / width)
    gain = lax.rsqrt(meansq - mean * mean + epsilon)
    entries = table[...]
    pieces = []
    for _ in range(3):
        piece = entries.astype(jnp.bfloat16).astype(jnp.float32)
        entries = entries - piece
        pieces.append(piece)
    split = jnp.concatenate(pieces, axis=0).astype(jnp.bfloat16)

    def lookup(kind):
        onehot = chosen_rows(turned[:, 2:3], steps, kind, 3).astype(jnp.bfloat16)
        return jnp.dot(onehot, split, preferred_element_type=jnp.float32)

    normed = (values[...].astype(jnp.float32) - mean) * gain
    out[...] = (normed * (1.0 + lookup(0)) + lookup(1)).astype(jnp.bfloat16)


def modulate(plan, at_core, step_ids, moments, values, table, width):
    tokens, local_width = values.shape
    size = 2 * LANES
    count = local_width // size
    columns = pl.BlockSpec((tokens, size), lambda i, at: (0, i))
    return gridded(
        functools.partial(modulate_kernel, width),
        plan,
        count,
        [
            pl.BlockSpec((1, tokens), lambda i, at: (0, 0)),
            pl.BlockSpec((8, tokens), lambda i, at: (0, 0)),
            columns,
            pl.BlockSpec((table.shape[0], size), lambda i, at: (0, at[at_core] * count + i)),
        ],
        columns,
        jax.ShapeDtypeStruct(values.shape, jnp.bfloat16),
        step_ids,
        moments,
        values,
        table,
    )


def pipeline(count, make_part, stage, hooks, extras, later, finish):
    own, sent1, came1, came2, came3, owned = {}, {}, {}, {}, {}, {}
    due2, due3 = {}, {}
    for j in range(count):
        due2[j] = max(j + 1, min(j + (LAG if j < LAST else 1), count))
        due3[j] = due2[j] + 1

    def begin(k, raw):
        own[k], sent1[k] = make_part(k, raw)
        came1[k] = lax.ppermute(sent1[k], "dp", swap(8, 2))

    begin(0, stage(0))
    if GATE:
        begin(1, stage(1))
    else:
        ready, raw = lax.optimization_barrier((hooks[0][0](), stage(1)))
        hooks = {0: (lambda: ready, hooks[0][1])}
        begin(1, raw)
    for k in range(max(due3.values()) + 1):
        now2 = [j for j in range(count) if due2[j] == k]
        now3 = [j for j in range(count) if due3[j] == k]
        wanted = {}
        if k < count:
            wanted["came1"] = came1[k]
        if k + 1 < count:
            wanted["sent1"] = sent1[k + 1]
        if k in hooks:
            wanted["more"] = hooks[k][0]()
        if k in extras:
            wanted["extra"] = extras[k][0]()
        if k in DOUBLES:
            wanted["next1"] = came1[k + 1]
        wanted = lax.optimization_barrier(wanted)
        if k in hooks and not HOOK_LATE:
            hooks[k][1](wanted["more"])
        if k in extras:
            extras[k][1](wanted["extra"])
        if k in DOUBLES:
            came1[k + 1] = wanted["next1"]
        if k + 2 < count and k + 2 not in later:
            raw, _ = lax.optimization_barrier((stage(k + 2), wanted["came1"]))
            begin(k + 2, raw)
            wanted, _ = lax.optimization_barrier((wanted, sent1[k + 2]))
        ahead = []
        if k < count:
            came1[k] = wanted["came1"]
            sent = add_sums(own[k], came1[k])
            ahead.append(sent)
            came2[k] = lax.ppermute(sent, "dp", swap(8, 4))
        rest = {"came2": [came2[j] for j in now2]}
        rest, _ = lax.optimization_barrier((rest, wanted["came1"] if FIRST and k < count else ahead))
        if EARLY and k + 2 < count and k + 2 in later:
            raw, _ = lax.optimization_barrier((stage(k + 2), tuple(ahead)))
            begin(k + 2, raw)
            rest, _ = lax.optimization_barrier((rest, sent1[k + 2]))
        for j, came in zip(now2, rest["came2"]):
            owned[j], sent = total_sums(own[j], came1[j], came)
            ahead.append(sent)
            came3[j] = lax.ppermute(sent, "dp", swap(8))
        ended, _ = lax.optimization_barrier(([came3[j] for j in now3], tuple(ahead)))
        for j, came in zip(now3, ended):
            finish(j, owned[j], came)
        if not EARLY and k + 2 < count and k + 2 in later:
            raw, _ = lax.optimization_barrier((stage(k + 2), tuple(ahead)))
            begin(k + 2, raw)
        if k in hooks and HOOK_LATE:
            more, _ = lax.optimization_barrier((wanted["more"], sent1[k + 2] if HOOK_LATE == 1 else tuple(ahead)))
            hooks[k][1](more)


def unpacked(message):
    rows = message.shape[0] - TAIL
    return message[:rows].astype(jnp.float32) * jnp.exp2(message[rows : rows + 1].astype(jnp.float32))


def in_order(own, other):
    side = lax.axis_index("dp") % 2
    return jnp.where(side == 0, own, other), jnp.where(side == 0, other, own)


def assemble(done, shared, scale):
    core = lax.axis_index("tensor")
    half = ROW_DEV // 2
    cores = []
    for which in range(2):
        mine = done[which::2]
        pieces = []
        if shared:
            pieces.append(mine[0][0] + mine[0][1])
            mine = mine[1:]
        ordered = [in_order(*pair) for pair in mine]
        head = [ordered[0][0][:, :half], ordered[0][1][:, :half]]
        ordered[0] = (ordered[0][0][:, half:], ordered[0][1][:, half:])
        pieces = head + pieces + [pair[0] for pair in ordered] + [pair[1] for pair in ordered]
        cores.append(jnp.concatenate(pieces, axis=1))
    left = jnp.where(core == 0, cores[0], cores[1])
    right = jnp.where(core == 0, cores[1], cores[0])
    return jnp.concatenate([left, right], axis=1) * scale


def body(hidden, attn_out, step_ids, modulation):
    token_count = hidden.shape[0]
    local_width = hidden.shape[1]
    parts_tp = lax.axis_size("tensor")
    dp = lax.axis_size("dp")
    width = local_width * parts_tp
    tokens = token_count * dp
    factor = 2.0 / tokens
    core_swap = swap(2)
    side = lax.axis_index("dp") % 2
    place = lax.axis_index("dp") // 2
    blocks = local_width // LANES
    store = {}

    order = [place ^ 3, place ^ 1, place ^ 2, place]
    arrived = [jnp.where(index // 2 == side, 2 + index % 2, index % 2) for index in order]

    def owned_blocks(which, common):
        rest = (blocks - 2 - common) // 2
        return [which] + [2 + common + which * rest + i for i in range(rest)]

    common = COMMON
    attn_mine = owned_blocks(side, common)
    attn_theirs = owned_blocks(1 - side, common)
    qkv_mine = owned_blocks(side, 0)
    qkv_theirs = owned_blocks(1 - side, 0)
    first = 4

    shared = [2 + i for i in range(common)]
    core = lax.axis_index("tensor")

    lists = ([core], order, arrived, shared, attn_mine, [side] + attn_theirs, qkv_mine, [side] + qkv_theirs)
    at_core, at_order, at_arrived, at_shared, at_attn, at_attn_theirs, at_qkv, at_qkv_theirs = (
        sum(len(entries) for entries in lists[:index]) for index in range(len(lists))
    )
    plan = jnp.stack([jnp.asarray(entry, jnp.int32) for entries in lists for entry in entries])

    ids = step_ids.reshape(1, token_count)
    table = modulation.reshape(2 * modulation.shape[0], width)

    attn_rows = turn(plan, attn_out, at_order)
    attn = attn_out
    attn_far = lax.ppermute(attn, "tensor", core_swap)
    if not PICK_LATE:
        store["attn_pair"] = lax.ppermute(pick(plan, attn, at_attn_theirs, (1, 1, len(attn_theirs) - 1)), "dp", swap(dp))

    def qkv_input():
        values, _ = lax.optimization_barrier((hidden, sent1_gate[0]))
        moments = lax.psum(stats(values), "tensor")
        return modulate(plan, at_core, ids, moments, values, table, width)

    def qkv_ready(mod):
        store["mod"] = mod
        store["pieces"] = {}
        store["far_pieces"] = {}
        for index in range(len(PIECES)):
            if index:
                mod, _ = lax.optimization_barrier((mod, message))
            message = pick(plan, mod, at_qkv_theirs + sum(PIECES[:index]), (PIECES[index],) if index else (1, 1, PIECES[0] - 2))
            store["pieces"][index] = lax.ppermute(message, "dp", swap(dp))
        store["mod_far"] = lax.ppermute(store["mod"], "tensor", core_swap)
        store["rows"] = turn(plan, store["mod"], at_order)

    sent1_gate = []
    extras = {}
    if ROWS_AT:
        extras[ROWS_AT] = (lambda: store["rows"], lambda value: store.update(rows=value))
    hooks = {0: (qkv_input, qkv_ready)}

    count = len(attn_mine)
    pair_sizes = (PIECES[0] - 1,) + PIECES[1:]

    def stage(k):
        needed = []
        for kind, far, first, size in CHUNKS[k]:
            if kind == "shared":
                needed.append(attn_far if far else attn)
            elif kind == "attn":
                needed.append(fetched("attn", far, 0))
            else:
                needed.append([fetched("qkv", far, index) for index, _, _ in qkv_pieces(first, size)])
        return needed

    def fetched(kind, far, index):
        if kind == "attn":
            near = store["attn_pair"]
        else:
            near = store["pieces"][index]
        if not far:
            return near
        key = (kind, index)
        if key not in store:
            store[key] = lax.ppermute(store.get(("near",) + key, near), "tensor", core_swap)
        return store[key]

    def landed(kind, far, index, value):
        if not far and ("near", kind, index) not in store:
            store["near", kind, index] = value
            store[kind, index] = lax.ppermute(value, "tensor", core_swap)
            if index == 0:
                store["other_" + kind] = turn(plan, value, at_arrived)

    def qkv_pieces(first, size):
        held = []
        for index, length in enumerate(pair_sizes):
            start = sum(pair_sizes[:index])
            low, high = max(first, start), min(first + size, start + length)
            if low < high:
                held.append((index, low - start, high - low))
        return held

    def make_part(k, raw):
        columns, others = [], []
        rows, other_rows = attn_rows, None
        for (kind, far, first, size), held in zip(CHUNKS[k], raw):
            if kind == "shared":
                columns.append((held, at_shared + first, size))
            elif kind == "attn":
                landed("attn", far, 0, held)
                columns.append((attn_far if far else attn, at_attn + first, size))
                others.append((held, 1 + first, size))
                other_rows = store["other_attn"]
            else:
                for (index, _, _), piece in zip(qkv_pieces(first, size), held):
                    landed("qkv", far, index, piece)
                rows, other_rows = store["rows"], store["other_qkv"]
                columns.append((store["mod_far" if far else "mod"], at_qkv + first, size))
                for (index, start, length), piece in zip(qkv_pieces(first, size), held):
                    others.append((piece, start + (1 if index == 0 else 0), length))
        result = gram(plan, rows, columns, other_rows, others)
        if k == 0 and PICK_LATE:
            late, _ = lax.optimization_barrier((attn, result[1]))
            store["attn_pair"] = lax.ppermute(pick(plan, late, at_attn_theirs, (1, 1, len(attn_theirs) - 1)), "dp", swap(dp))
        if k == GATE:
            sent1_gate.append(result[1])
        return result

    done = {}
    results = {}

    def finish(k, own, came):
        values = unpacked(came)
        at = 0
        for kind, far, first, size in CHUNKS[k]:
            end = at + size * LANES
            done[kind, far, first] = (own[:, at:end], values[:, at:end])
            at = end
        kinds = [entry[0] for parts in CHUNKS for entry in parts if entry[0] != "qkv"]
        if "out" not in results and len([key for key in done if key[0] != "qkv"]) == len(kinds):
            joined = [gathered(kind, far) for kind in ("shared", "attn") for far in (False, True)]
            results["out"] = assemble(joined, True, factor)

    def gathered(kind, far):
        parts = [done[key] for key in sorted(key for key in done if key[:2] == (kind, far))]
        return tuple(jnp.concatenate(pieces, axis=1) for pieces in zip(*parts))

    pipeline(len(CHUNKS), make_part, stage, hooks, extras, LATER, finish)
    qkv_rows = assemble([gathered("qkv", far) for far in (False, True)], False, factor)
    return (qkv_rows, results["out"])


def solution(mesh):
    lined = mesh.shape["dp"] == 8 and mesh.shape["tensor"] == 2
    return jax.shard_map(
        body if lined else plain_body,
        mesh=mesh,
        in_specs=(
            P(("groups", "dp"), "tensor"),
            P(("groups", "dp"), "tensor"),
            P(("groups", "dp")),
            P("groups", None, None),
        ),
        out_specs=(P(("groups", "dp", "tensor"), None), P(("groups", "dp", "tensor"), None)),
        check_vma=False,
    )
```
